32 devices in a mesh: dp: 8 (over z, x), tensor: 4 (over y, core).
Axes of the slice: x: 2, y: 2, z: 4, core: 2. Of those that a mesh axis runs over, the one named last changes fastest.
Arguments:
- tokens: bfloat16 [8192, 640], P(('dp', 'tensor')), may hold values from -6 to 6
- segments: int32 [8192], P(('dp', 'tensor')), may hold values from 0 to 31, as said below
- query_weight: bfloat16 [640, 1024], P('dp', 'tensor'), may hold values from -0.25 to 0.25
- keyvalue_weight: bfloat16 [640, 512], P('dp'), may hold values from -0.25 to 0.25
- output_weight: bfloat16 [1024, 640], P('tensor', 'dp'), may hold values from -0.1875 to 0.1875
- gate_weight: bfloat16 [640, 2048], P('dp', 'tensor'), may hold values from -0.25 to 0.25
- up_weight: bfloat16 [640, 2048], P('dp', 'tensor'), may hold values from -0.25 to 0.25
- down_weight: bfloat16 [2048, 640], P('tensor', 'dp'), may hold values from -0.125 to 0.125
- norm_gains: float32 [4, 640], replicated, may hold values from 0.5 to 1.5
- headnorm_gains: float32 [2, 256], replicated, may hold values from 0.5 to 1.5
- cotangent: bfloat16 [8192, 640], P(('dp', 'tensor')), may hold values from -6 to 6
Outputs:
- output: bfloat16 [8192, 640], P(('dp', 'tensor'))
- grad_tokens: float32 [8192, 640], P(('dp', 'tensor'))
- grad_query_weight: float32 [640, 1024], P('dp', 'tensor')
- grad_keyvalue_weight: float32 [640, 512], P('dp', 'tensor')
- grad_output_weight: float32 [1024, 640], P('tensor', 'dp')
- grad_gate_weight: float32 [640, 2048], P('dp', 'tensor')
- grad_up_weight: float32 [640, 2048], P('dp', 'tensor')
- grad_down_weight: float32 [2048, 640], P('tensor', 'dp')
- grad_norm_gains: float32 [4, 640], P('tensor', 'dp')
- grad_headnorm_gains: float32 [2, 256], P(None, ('dp', 'tensor'))
The draws below stay inside these ranges and needn't reach their ends.
Inputs may be any that keep to these rules, and one draw needn't show every extreme that they name: `segments`: sequence s (tokens s * 1024 to (s + 1) * 1024 - 1) holds exactly four documents in order, numbered 4 s to 4 s + 3; the second begins before position 256 and ends after position 768 of its sequence.
All inputs are finite; a program needn't handle non-finite values.
Results may differ from the reference program's by a relative error of at most 0.024.
Values may be sent and summed in bfloat16 or wider, within the bound.
A program may use at most 128 MiB of HBM per device.

```python
import jax
import jax.numpy as jnp
from jax import lax

D = 640
H = 4
HD = 256
FF = 2048
LEN = 1024
TOKENS = 8192


def draw_segments(key, part):
    key = jax.random.fold_in(key, 11)
    sequence_count = TOKENS // LEN
    subkeys = jax.random.split(key, 3)
    opening = jax.random.randint(subkeys[0], (sequence_count,), max(1, LEN // 32), LEN // 4)
    closing = jax.random.randint(subkeys[1], (sequence_count,), 3 * LEN // 4 + 1, 7 * LEN // 8)
    boundary = closing + jax.random.randint(subkeys[2], (sequence_count,), 1, LEN - closing)
    places = jnp.arange(LEN, dtype=jnp.int32)[None, :]
    local_ids = (places >= opening[:, None]).astype(jnp.int32) + (places >= closing[:, None]).astype(jnp.int32) + (places >= boundary[:, None]).astype(jnp.int32)
    numbered = local_ids + 4 * jnp.arange(sequence_count, dtype=jnp.int32)[:, None]
    return numbered.reshape(-1).astype(jnp.int32)


def levels(own_key, shape, cuts, least, high):
    loudness = 1.0
    for dim, blocks in cuts:
        heights = jax.random.uniform(jax.random.fold_in(jax.random.fold_in(own_key, 6), dim), (blocks,), jnp.float32, least / len(cuts), high / len(cuts))
        loudness = loudness * jnp.repeat(jnp.exp(heights), shape[dim] // blocks).reshape((-1,) + (1,) * (len(shape) - 1 - dim))
    return loudness


def noise(stream_key, shape, spread, bound, cuts=(), kind=jnp.bfloat16):
    values = jax.random.normal(stream_key, shape, jnp.float32) * spread
    if len(cuts) > 0:
        values = levels(stream_key, shape, cuts, -0.22, 0.18) * values
    return jnp.clip(values, min=-bound, max=bound).astype(kind)


def setup_inputs(seed: int = 0) -> dict:
    arg_keys = jax.random.split(jax.random.key(seed), 12)
    tokens = noise(arg_keys[0], (TOKENS, D), 1.0, 6.0, ((0, 32),))
    segments = draw_segments(jax.random.fold_in(arg_keys[11], 71), 0)
    query_weight = noise(arg_keys[2], (D, H * HD), D ** -0.5, 0.25, ((0, 8), (1, 4)))
    keyvalue_weight = noise(arg_keys[3], (D, 2 * HD), D ** -0.5, 0.25, ((0, 8),))
    output_weight = noise(arg_keys[4], (H * HD, D), (H * HD) ** -0.5, 0.1875, ((0, 4), (1, 8)))
    gate_weight = noise(arg_keys[5], (D, FF), D ** -0.5, 0.25, ((0, 8), (1, 4)))
    up_weight = noise(arg_keys[6], (D, FF), D ** -0.5, 0.25, ((0, 8), (1, 4)))
    down_weight = noise(arg_keys[7], (FF, D), FF ** -0.5, 0.125, ((0, 4), (1, 8)))
    norm_gains = jnp.clip(1.0 + 0.1 * jax.random.normal(arg_keys[8], (4, D), jnp.float32), 0.5, 1.5)
    headnorm_gains = jnp.clip(1.0 + 0.1 * jax.random.normal(arg_keys[9], (2, HD), jnp.float32), 0.5, 1.5)
    cotangent = noise(arg_keys[10], (TOKENS, D), 1.0, 6.0, ((0, 32),))
    return {"tokens": tokens, "segments": segments, "query_weight": query_weight, "keyvalue_weight": keyvalue_weight, "output_weight": output_weight, "gate_weight": gate_weight, "up_weight": up_weight, "down_weight": down_weight, "norm_gains": norm_gains, "headnorm_gains": headnorm_gains, "cotangent": cotangent}


@jax.custom_vjp
def low(v):
    return lax.optimization_barrier(v.astype(jnp.bfloat16)).astype(jnp.float32)

@jax.custom_vjp
def low_back(v):
    return v

def low_keep(v):
    return (low(v), None)

def low_pass(kept, grad):
    return (grad,)

def back_keep(v):
    return (v, None)

def back_low(kept, grad):
    return (low(grad),)
low.defvjp(low_keep, low_pass)
low_back.defvjp(back_keep, back_low)
epsilon = 1e-06
rope_base = 1000000.0
score_scale = 0.0625
highest_precision = lax.Precision.HIGHEST

def product(left_side, right_side):
    return jnp.dot(left_side, right_side, precision=highest_precision, preferred_element_type=jnp.float32)

def norm_rows(values, scaling):
    return values * lax.rsqrt(lax.optimization_barrier(jnp.mean(values * values, axis=-1, keepdims=True)) + epsilon) * scaling

def angles(length, head_width):
    halfway = head_width // 2
    places = jnp.arange(length, dtype=jnp.float32)[:, None]
    frequency = rope_base ** (-2.0 * jnp.arange(halfway, dtype=jnp.float32) / head_width)
    phases = places * frequency[None, :]
    return (jnp.cos(phases), jnp.sin(phases))

def rotate(values, cosine_table, sine_table):
    halfway = values.shape[-1] // 2
    leading = values[..., :halfway]
    trailing = values[..., halfway:]
    return jnp.concatenate([leading * cosine_table - trailing * sine_table, trailing * cosine_table + leading * sine_table], axis=-1)

def attend_head(query_raw, keyvalue_raw, segment_ids, query_gain, key_gain, cosine_table, sine_table):
    head_width = query_gain.shape[0]
    query_rows = low(rotate(norm_rows(query_raw, query_gain), cosine_table, sine_table) * score_scale)
    keyvalue = low_back(keyvalue_raw)
    key_rows = low(rotate(norm_rows(keyvalue[:, :head_width], key_gain), cosine_table, sine_table))
    value_rows = low(keyvalue[:, head_width:])
    scores = low_back(jnp.dot(query_rows, key_rows.T, precision=highest_precision))
    places = jnp.arange(query_raw.shape[0])
    allowed = (places[None, :] <= places[:, None]) & (segment_ids[:, None] == segment_ids[None, :])
    scores = jnp.where(allowed, scores, -jnp.inf)
    row_peak = lax.optimization_barrier(jnp.max(scores, axis=-1, keepdims=True))
    raised = jnp.exp(scores - row_peak)
    weights_p = low(raised / lax.optimization_barrier(jnp.sum(raised, axis=-1, keepdims=True)))
    return low(low_back(jnp.dot(weights_p, value_rows, precision=highest_precision)))

def layer_sequence(weights, tokens_seq, segment_ids):
    query_weight, keyvalue_weight, output_weight, gate_weight, up_weight, down_weight, norm_gains, headnorm_gains = weights
    length = tokens_seq.shape[0]
    head_width = headnorm_gains.shape[1]
    heads = query_weight.shape[1] // head_width
    cosine_table, sine_table = angles(length, head_width)
    normed_in = low(norm_rows(tokens_seq, norm_gains[0]))
    query_raw = low_back(product(normed_in, query_weight))
    keyvalue_raw = product(normed_in, keyvalue_weight)
    attended = jnp.concatenate([attend_head(query_raw[:, head_id * head_width:(head_id + 1) * head_width], keyvalue_raw, segment_ids, headnorm_gains[0], headnorm_gains[1], cosine_table, sine_table) for head_id in range(heads)], axis=1)
    branch = low_back(product(attended, output_weight))
    middle = tokens_seq + norm_rows(branch, norm_gains[1])
    normed_mid = low(norm_rows(middle, norm_gains[2]))
    gating = low_back(product(normed_mid, gate_weight))
    upward = low_back(product(normed_mid, up_weight))
    hidden = low(jax.nn.gelu(gating, approximate=True) * upward)
    ffn_out = low_back(product(hidden, down_weight))
    return middle + norm_rows(ffn_out, norm_gains[3])

def reference(tokens, segments, query_weight, keyvalue_weight, output_weight, gate_weight, up_weight, down_weight, norm_gains, headnorm_gains, cotangent):
    floats = tuple((array.astype(jnp.float32) for array in (tokens, query_weight, keyvalue_weight, output_weight, gate_weight, up_weight, down_weight, norm_gains, headnorm_gains)))

    def forward(tokens_f, *weights):

        def per_sequence(paired):
            return jax.checkpoint(lambda seq_tokens, seq_ids: layer_sequence(weights, seq_tokens, seq_ids))(paired[0], paired[1])
        stacked = lax.map(per_sequence, (tokens_f.reshape(-1, LEN, tokens_f.shape[1]), segments.reshape(-1, LEN)))
        return stacked.reshape(tokens_f.shape)
    result, pull_back = jax.vjp(forward, *floats)
    grads = pull_back(cotangent.astype(jnp.float32))
    return (result.astype(jnp.bfloat16), grads[0], grads[1], grads[2], grads[3], grads[4], grads[5], grads[6], grads[7], grads[8])
```

```python
import functools

import jax
import jax.numpy as jnp
from jax import lax
from jax.experimental import pallas as pl
from jax.experimental.pallas import tpu as pltpu
from jax.sharding import PartitionSpec as P

epsilon = 1e-06
rope_base = 1000000.0
score_scale = 0.0625
MESH = pl.DeviceIdType.MESH
chunk_count = 4
vmem_bytes = 56 * 2**20
in_vmem = pl.BlockSpec(memory_space=pltpu.VMEM)


def norm_rows(values, scaling):
    return values * lax.rsqrt(jnp.mean(values * values, axis=-1, keepdims=True) + epsilon) * scaling


def norm_pull(values, scaling, grad):
    inverse = lax.rsqrt(jnp.mean(values * values, axis=-1, keepdims=True) + epsilon)
    scaled = grad * scaling
    inner = jnp.mean(values * scaled, axis=-1, keepdims=True)
    pulled = inverse * scaled - values * (inverse * inverse * inverse * inner)
    return pulled, jnp.sum(grad * values * inverse, axis=0, keepdims=True)


def angles(length, head_width):
    halfway = head_width // 2
    places = jnp.arange(length, dtype=jnp.float32)[:, None]
    frequency = rope_base ** (-2.0 * jnp.arange(halfway, dtype=jnp.float32) / head_width)
    phases = places * frequency[None, :]
    return (jnp.cos(phases), jnp.sin(phases))


def rotate(values, cosine_table, sine_table):
    halfway = values.shape[-1] // 2
    leading = values[..., :halfway]
    trailing = values[..., halfway:]
    return jnp.concatenate(
        [
            leading * cosine_table - trailing * sine_table,
            trailing * cosine_table + leading * sine_table,
        ],
        axis=-1,
    )


def activate(gating, upward):
    return jax.nn.gelu(gating, approximate=True) * upward


def dot_rows(left_side, right_side):
    return jnp.dot(left_side, right_side, preferred_element_type=jnp.float32)


def dot_inner(left_side, right_side):
    return lax.dot_general(
        left_side, right_side, (((1,), (1,)), ((), ())), preferred_element_type=jnp.float32
    )


def dot_outer(left_side, right_side):
    return lax.dot_general(
        left_side, right_side, (((0,), (0,)), ((), ())), preferred_element_type=jnp.float32
    )


def send(source, target, send_sem, recv_sem, device):
    return pltpu.make_async_remote_copy(
        src_ref=source,
        dst_ref=target,
        send_sem=send_sem,
        recv_sem=recv_sem,
        device_id=device,
        device_id_type=MESH,
    )


def tensor_peers():
    me = lax.axis_index("tensor")
    chip = me // 2
    core = me % 2
    mate = chip * 2 + 1 - core
    across = (1 - chip) * 2 + core
    diagonal = (1 - chip) * 2 + 1 - core
    return me, mate, across, diagonal


def ring_place(index, count):
    odd = index % 2
    return (index // 2) * (1 - odd) + (count - 1 - index // 2) * odd


def ring_index(place, count):
    back = place // (count // 2)
    return (2 * place) * (1 - back) + (2 * (count - 1 - place) + 1) * back


def greet(targets):
    barrier = pltpu.get_barrier_semaphore()
    for target in targets:
        pl.semaphore_signal(barrier, inc=1, device_id=target, device_id_type=MESH)
    pl.semaphore_wait(barrier, len(targets))


def call(kernel, arguments, outputs, scratch, collective_id):
    return pl.pallas_call(
        kernel,
        out_shape=outputs,
        in_specs=[in_vmem] * len(arguments),
        out_specs=[in_vmem] * len(outputs),
        scratch_shapes=scratch,
        compiler_params=pltpu.CompilerParams(
            collective_id=collective_id, has_side_effects=True, vmem_limit_bytes=vmem_bytes
        ),
    )(*arguments)


class Spread:
    def __init__(self, gathered, send_sems, recv_sems, rows):
        self.gathered, self.send_sems, self.recv_sems, self.rows = gathered, send_sems, recv_sems, rows
        self.me, self.mate, self.across, self.diagonal = tensor_peers()
        self.sent = []

    def copy(self, flow, owner, chunk, device):
        part = self.gathered.at[owner, pl.ds(chunk * self.rows, self.rows)]
        return send(
            part, part, self.send_sems.at[flow, chunk], self.recv_sems.at[flow, chunk], {"tensor": device}
        )

    def give(self, chunk):
        for flow, device in ((0, self.across), (1, self.mate)):
            copy = self.copy(flow, self.me, chunk, device)
            copy.start()
            self.sent.append(copy)

    def forward(self, chunk):
        self.copy(0, self.across, chunk, self.across).wait_recv()
        copy = self.copy(2, self.across, chunk, self.mate)
        copy.start()
        self.sent.append(copy)

    def finish(self, chunks):
        for chunk in range(chunks):
            self.copy(1, self.mate, chunk, self.mate).wait_recv()
            self.copy(2, self.diagonal, chunk, self.mate).wait_recv()
        for copy in self.sent:
            copy.wait_send()


def opening_kernel(
    count, tokens, segments, gains, shard, rows_all, segment_all, full, send_sems, recv_sems, seg_send, seg_recv, ring_send, ring_recv
):
    me, mate, across, diagonal = tensor_peers()
    mine = lax.axis_index("dp")
    place = ring_place(mine, count)
    right = ring_index((place + 1) % count, count)
    left = ring_index((place + count - 1) % count, count)
    greet([{"tensor": mate}, {"tensor": across}, {"tensor": diagonal}, {"dp": right}, {"dp": left}])
    full[mine] = shard[...]
    segment_all[me] = segments[...]
    half = shard.shape[1] // 2
    last = count // 2 - 1

    def ring_copy(way, step, owner):
        device = {"dp": left if way else right}
        part = full.at[owner]
        if step == last:
            part = full.at[owner, :, pl.ds(half * way, half)]
        return send(part, part, ring_send.at[way, step], ring_recv.at[way, step], device)

    def ring_owner(way, step):
        shift = step if way else count - step
        return ring_index((place + shift) % count, count)

    ring_sent = []

    def ring_start(step):
        for way in (0, 1):
            if step > 0:
                ring_copy(way, step - 1, ring_owner(way, step)).wait_recv()
            if step <= last:
                copy = ring_copy(way, step, ring_owner(way, step))
                copy.start()
                ring_sent.append(copy)

    ring_start(0)
    spread = Spread(rows_all, send_sems, recv_sems, tokens.shape[0] // chunk_count)
    for chunk in range(chunk_count):
        rows = pl.ds(chunk * spread.rows, spread.rows)
        normed = norm_rows(tokens[rows, :].astype(jnp.float32), gains[0:1, :])
        rows_all[me, rows, :] = normed.astype(jnp.bfloat16)
        spread.give(chunk)
    seg_sent = []
    for flow, device in enumerate((mate, across, diagonal)):
        part = segment_all.at[me]
        copy = send(part, part, seg_send.at[flow], seg_recv.at[flow], {"tensor": device})
        copy.start()
        seg_sent.append(copy)
    for chunk in range(chunk_count):
        spread.forward(chunk)
    for step in range(1, last + 2):
        ring_start(step)
    spread.finish(chunk_count)
    for flow, device in enumerate((mate, across, diagonal)):
        part = segment_all.at[device]
        send(part, part, seg_send.at[flow], seg_recv.at[flow], {"tensor": device}).wait_recv()
    for copy in seg_sent + ring_sent:
        copy.wait_send()


def opening(tokens, segments, gains, shard, count):
    rows, width = tokens.shape
    return call(
        functools.partial(opening_kernel, count),
        (tokens, segments, gains, shard),
        [
            jax.ShapeDtypeStruct((4, rows, width), jnp.bfloat16),
            jax.ShapeDtypeStruct((4,) + segments.shape, jnp.int32),
            jax.ShapeDtypeStruct((count,) + shard.shape, jnp.bfloat16),
        ],
        [
            pltpu.SemaphoreType.DMA((3, chunk_count)),
            pltpu.SemaphoreType.DMA((3, chunk_count)),
            pltpu.SemaphoreType.DMA((3,)),
            pltpu.SemaphoreType.DMA((3,)),
            pltpu.SemaphoreType.DMA((2, count // 2)),
            pltpu.SemaphoreType.DMA((2, count // 2)),
        ],
        0,
    )


def joint_kernel(row_map, extra_count, row_count, sum_count, spreads, *refs):
    refs = list(refs)

    def take(number):
        taken = refs[:number]
        del refs[:number]
        return taken

    (partial,) = take(1)
    extras = take(extra_count)
    (gains,) = take(1)
    gathered = take(1)[0] if spreads else None
    row_outs = take(row_count)
    sum_outs = take(sum_count)
    near, outgoing, far, send_sems, recv_sems = take(5)
    if spreads:
        spread_send, spread_recv = take(2)
    me, mate, across, diagonal = tensor_peers()
    rows_each = partial.shape[1] // chunk_count
    greet([{"tensor": mate}, {"tensor": across}])

    def near_copy(flow, chunk):
        owner = mate if flow else diagonal
        part = pl.ds(chunk * rows_each, rows_each)
        return send(
            partial.at[owner, part], near.at[flow, part], send_sems.at[flow, chunk], recv_sems.at[flow, chunk], {"tensor": mate}
        )

    def far_copy(chunk):
        part = pl.ds(chunk * rows_each, rows_each)
        return send(outgoing.at[part], far.at[part], send_sems.at[2, chunk], recv_sems.at[2, chunk], {"tensor": across})

    for flow in (0, 1):
        for chunk in range(chunk_count):
            near_copy(flow, chunk).start()
    for chunk in range(chunk_count):
        part = pl.ds(chunk * rows_each, rows_each)
        near_copy(0, chunk).wait_recv()
        total = partial[across, part, :].astype(jnp.float32) + near[0, part, :].astype(jnp.float32)
        outgoing[part, :] = total.astype(jnp.bfloat16)
        far_copy(chunk).start()
    if spreads:
        spread = Spread(gathered, spread_send, spread_recv, rows_each)
    sums = None
    for chunk in range(chunk_count):
        part = pl.ds(chunk * rows_each, rows_each)
        near_copy(1, chunk).wait_recv()
        total = partial[me, part, :].astype(jnp.float32) + near[1, part, :].astype(jnp.float32)
        far_copy(chunk).wait_recv()
        total = total + far[part, :].astype(jnp.float32)
        given, rows_out, sums_out = row_map(total, [extra[part, :] for extra in extras], gains)
        if spreads:
            gathered[me, part, :] = given.astype(jnp.bfloat16)
            spread.give(chunk)
        for ref, value in zip(row_outs, rows_out):
            ref[part, :] = value.astype(ref.dtype)
        sums = sums_out if sums is None else [held + new for held, new in zip(sums, sums_out)]
        if spreads and chunk > 0:
            spread.forward(chunk - 1)
    for ref, value in zip(sum_outs, sums):
        ref[...] = value
    if spreads:
        spread.forward(chunk_count - 1)
        spread.finish(chunk_count)
    for chunk in range(chunk_count):
        near_copy(0, chunk).wait_send()
        near_copy(1, chunk).wait_send()
        far_copy(chunk).wait_send()


def joint(row_map, partial, extras, gains, row_types, sum_count, spreads, collective_id):
    rows, width = partial.shape[0] // 4, partial.shape[1]
    outputs = []
    if spreads:
        outputs.append(jax.ShapeDtypeStruct((4, rows, width), jnp.bfloat16))
    outputs += [jax.ShapeDtypeStruct((rows, width), kind) for kind in row_types]
    outputs += [jax.ShapeDtypeStruct((1, width), jnp.float32)] * sum_count
    scratch = [
        pltpu.VMEM((2, rows, width), jnp.bfloat16),
        pltpu.VMEM((rows, width), jnp.bfloat16),
        pltpu.VMEM((rows, width), jnp.bfloat16),
        pltpu.SemaphoreType.DMA((3, chunk_count)),
        pltpu.SemaphoreType.DMA((3, chunk_count)),
    ]
    if spreads:
        scratch += [pltpu.SemaphoreType.DMA((3, chunk_count))] * 2
    found = list(call(
        functools.partial(joint_kernel, row_map, len(extras), len(row_types), sum_count, spreads),
        (partial.reshape(4, rows, width),) + tuple(extras) + (gains,),
        outputs,
        scratch,
        collective_id,
    ))
    if spreads:
        found[0] = found[0].reshape(4 * rows, width)
    return found


def branch_map(branch, extras, gains):
    middle = extras[0].astype(jnp.float32) + norm_rows(branch, gains[1:2, :])
    return norm_rows(middle, gains[2:3, :]), [branch, middle], []


def ffn_map(ffn_out, extras, gains):
    middle, cotangent = extras
    outcome = middle + norm_rows(ffn_out, gains[3:4, :])
    grad_ffn, gain_last = norm_pull(ffn_out, gains[3:4, :], cotangent.astype(jnp.float32))
    return grad_ffn, [outcome], [gain_last]


def middle_map(grad_mid_normed, extras, gains):
    middle, branch, cotangent = extras
    pulled, gain_mid = norm_pull(middle, gains[2:3, :], grad_mid_normed)
    grad_middle = cotangent.astype(jnp.float32) + pulled
    grad_branch, gain_branch = norm_pull(branch, gains[1:2, :], grad_middle)
    return grad_branch, [grad_middle], [gain_branch, gain_mid]


def first_map(grad_first_normed, extras, gains):
    tokens, grad_middle = extras
    pulled, gain_first = norm_pull(tokens.astype(jnp.float32), gains[0:1, :], grad_first_normed)
    return None, [grad_middle + pulled], [gain_first]


def closing_kernel(count, split, shared, grads, summed, joined, slots_a, slots_b, staged, arrived, send_sems, recv_sems, tail_send, tail_recv):
    me = lax.axis_index("tensor")
    mine = lax.axis_index("dp")
    place = ring_place(mine, count)
    right = ring_index((place + 1) % count, count)
    left = ring_index((place + count - 1) % count, count)
    others = [(me + shift) % 4 for shift in (1, 2, 3)]
    greet([{"dp": right}, {"dp": left}] + [{"tensor": other} for other in others])
    width = grads.shape[2]
    ways = ((0, split), (split, width - split))

    def chunk_index(way, step):
        shift = 1 + step if way else 2 * count - 1 - step
        return ring_index((place + shift) % count, count)

    def ring_copy(way, step):
        slots = slots_b if way else slots_a
        start, size = ways[way]
        if step == 0:
            source = grads.at[chunk_index(way, 0), :, pl.ds(start, size)]
        else:
            source = slots.at[step - 1]
        return send(source, slots.at[step], send_sems.at[way, step], recv_sems.at[way, step], {"dp": left if way else right})

    for way in (0, 1):
        ring_copy(way, 0).start()
    for step in range(1, count):
        for way in (0, 1):
            slots = slots_b if way else slots_a
            start, size = ways[way]
            ring_copy(way, step - 1).wait_recv()
            total = slots[step - 1].astype(jnp.float32) + grads[chunk_index(way, step), :, pl.ds(start, size)].astype(jnp.float32)
            if step < count - 1:
                slots[step - 1] = total.astype(jnp.bfloat16)
                ring_copy(way, step).start()
            else:
                summed[:, pl.ds(start, size)] = total
    first, each, tail = shared
    for device in range(4):
        staged[device, :, pl.ds(0, each)] = summed[:, pl.ds(first + each * device, each)]
        staged[device, :, pl.ds(each, tail)] = summed[:, pl.ds(width - tail, tail)]
    tails = []
    for slot, other in enumerate(others):
        copy = send(staged.at[other], arrived.at[slot], tail_send.at[slot], tail_recv.at[slot], {"tensor": other})
        copy.start()
        tails.append(copy)
    total = staged[me]
    for slot in range(3):
        tails[slot].wait_recv()
        total = total + arrived[slot]
    joined[...] = total
    for copy in tails:
        copy.wait_send()
    for step in range(count - 1):
        for way in (0, 1):
            ring_copy(way, step).wait_send()


def closing(grads, shared, split, count):
    rows, width = grads.shape[1:]
    block = shared[1] + shared[2]
    return call(
        functools.partial(closing_kernel, count, split, shared),
        (grads,),
        [
            jax.ShapeDtypeStruct((rows, width), jnp.float32),
            jax.ShapeDtypeStruct((rows, block), jnp.float32),
        ],
        [
            pltpu.VMEM((count - 1, rows, split), jnp.bfloat16),
            pltpu.VMEM((count - 1, rows, width - split), jnp.bfloat16),
            pltpu.VMEM((4, rows, block), jnp.float32),
            pltpu.VMEM((3, rows, block), jnp.float32),
            pltpu.SemaphoreType.DMA((2, count - 1)),
            pltpu.SemaphoreType.DMA((2, count - 1)),
            pltpu.SemaphoreType.DMA((3,)),
            pltpu.SemaphoreType.DMA((3,)),
        ],
        5,
    )


def body(
    tokens,
    segments,
    query_weight,
    keyvalue_weight,
    output_weight,
    gate_weight,
    up_weight,
    down_weight,
    norm_gains,
    headnorm_gains,
    cotangent,
):
    head_width = headnorm_gains.shape[1]
    width = tokens.shape[1]
    hidden_width = gate_weight.shape[1]
    count = lax.axis_size("dp")
    own_rows = query_weight.shape[0]
    padded_rows = -(-own_rows // 16) * 16
    shard = jnp.concatenate(
        [query_weight, keyvalue_weight, output_weight.T, gate_weight, up_weight, down_weight.T], axis=1
    )
    shard = jnp.pad(shard, ((0, padded_rows - own_rows), (0, 0)))
    seg_tile = segments.reshape(-1, 128)
    seg_rows = seg_tile.shape[0]
    seg_tile = jnp.pad(seg_tile, ((0, 8 - seg_rows), (0, 0)))
    rows_all, segment_all, full = opening(tokens, seg_tile, norm_gains, shard, count)
    rows_all = rows_all.reshape(-1, width)
    segment_all = segment_all[:, :seg_rows].reshape(-1)
    full = full[:, :own_rows].reshape(width, -1)
    ends = [0, head_width, 3 * head_width, 4 * head_width, 4 * head_width + 2 * hidden_width, 4 * head_width + 3 * hidden_width]
    mixed_full = full[:, : ends[2]]
    output_full = full[:, ends[2] : ends[3]]
    pair_full = full[:, ends[3] : ends[4]]
    down_full = full[:, ends[4] : ends[5]]
    length = rows_all.shape[0]
    block_rows = min(512, length)
    cosine_table, sine_table = angles(length, head_width)

    def query_map(raw_values, scaling):
        return rotate(norm_rows(raw_values, scaling), cosine_table, sine_table) * score_scale

    def key_map(raw_values, scaling):
        return rotate(norm_rows(raw_values, scaling), cosine_table, sine_table)

    mixed_raw = dot_rows(rows_all, mixed_full)
    query_raw = mixed_raw[:, :head_width]
    keyvalue_raw = mixed_raw[:, head_width:]
    query_rows = query_map(query_raw, headnorm_gains[0]).astype(jnp.bfloat16)
    key_rows = key_map(keyvalue_raw[:, :head_width], headnorm_gains[1]).astype(jnp.bfloat16)
    value_rows = keyvalue_raw[:, head_width:].astype(jnp.bfloat16)

    def masked_scores(row_from, row_to):
        scores = dot_inner(query_rows[row_from:row_to], key_rows[:row_to])
        row_places = row_from + jnp.arange(row_to - row_from)
        key_places = jnp.arange(row_to)
        allowed = (key_places[None, :] <= row_places[:, None]) & (
            segment_all[row_from:row_to][:, None] == segment_all[:row_to][None, :]
        )
        return jnp.where(allowed, scores, -jnp.inf)

    pieces_out = []
    pieces_total = []
    for block_id in range(length // block_rows):
        row_from = block_id * block_rows
        row_to = row_from + block_rows
        scores = masked_scores(row_from, row_to)
        row_peak = jnp.max(scores, axis=-1, keepdims=True)
        raised = jnp.exp(scores - row_peak)
        row_total = jnp.sum(raised, axis=-1, keepdims=True)
        weights_low = (raised / row_total).astype(jnp.bfloat16)
        pieces_out.append(dot_rows(weights_low, value_rows[:row_to]).astype(jnp.bfloat16))
        pieces_total.append(row_peak + jnp.log(row_total))
    attended = jnp.concatenate(pieces_out, axis=0)
    log_totals = jnp.concatenate(pieces_total, axis=0)
    branch_partial = dot_inner(attended, output_full).astype(jnp.bfloat16)
    mid_all, branch, middle = joint(
        branch_map, branch_partial, (tokens,), norm_gains, (jnp.float32, jnp.float32), 0, True, 1
    )
    paired = dot_rows(mid_all, pair_full)
    gating = paired[:, :hidden_width]
    upward = paired[:, hidden_width:]
    hidden = activate(gating, upward).astype(jnp.bfloat16)
    ffn_partial = dot_inner(hidden, down_full).astype(jnp.bfloat16)
    grad_ffn_all, outcome, gain_last = joint(
        ffn_map, ffn_partial, (middle, cotangent), norm_gains, (jnp.bfloat16,), 1, True, 2
    )
    grad_hidden = dot_rows(grad_ffn_all, down_full)
    down_grad = dot_outer(grad_ffn_all, hidden).astype(jnp.bfloat16)
    ignored, pull_active = jax.vjp(activate, gating, upward)
    grad_gating, grad_upward = pull_active(grad_hidden)
    paired_low = jnp.concatenate(
        [grad_gating.astype(jnp.bfloat16), grad_upward.astype(jnp.bfloat16)], axis=1
    )
    mid_partial = dot_inner(paired_low, pair_full).astype(jnp.bfloat16)
    branch_all, grad_middle, gain_branch, gain_mid = joint(
        middle_map, mid_partial, (middle, branch, cotangent), norm_gains, (jnp.float32,), 2, True, 3
    )
    pair_grad = dot_outer(mid_all, paired_low).astype(jnp.bfloat16)
    output_grad = dot_outer(branch_all, attended).astype(jnp.bfloat16)
    grad_attended = dot_rows(branch_all, output_full).astype(jnp.bfloat16)
    grad_query_parts = []
    grad_keys = jnp.zeros((length, head_width), jnp.float32)
    grad_values = jnp.zeros((length, head_width), jnp.float32)
    for block_id in range(length // block_rows):
        row_from = block_id * block_rows
        row_to = row_from + block_rows
        scores = masked_scores(row_from, row_to)
        weights_full = jnp.exp(scores - log_totals[row_from:row_to])
        weights_low = weights_full.astype(jnp.bfloat16)
        grad_block = grad_attended[row_from:row_to]
        grad_weights = dot_inner(grad_block, value_rows[:row_to])
        row_inner = jnp.sum(weights_full * grad_weights, axis=-1, keepdims=True)
        grad_scores = (weights_full * (grad_weights - row_inner)).astype(jnp.bfloat16)
        grad_query_parts.append(dot_rows(grad_scores, key_rows[:row_to]))
        grad_keys = grad_keys.at[:row_to].add(dot_outer(grad_scores, query_rows[row_from:row_to]))
        grad_values = grad_values.at[:row_to].add(dot_outer(weights_low, grad_block))
    grad_query = jnp.concatenate(grad_query_parts, axis=0)
    ignored, pull_query = jax.vjp(query_map, query_raw, headnorm_gains[0])
    grad_query_raw, gain_query = pull_query(grad_query)
    ignored, pull_key = jax.vjp(key_map, keyvalue_raw[:, :head_width], headnorm_gains[1])
    grad_key_raw, gain_key = pull_key(grad_keys)
    mixed_low = jnp.concatenate([grad_query_raw, grad_key_raw, grad_values], axis=1).astype(jnp.bfloat16)
    first_partial = dot_inner(mixed_low, mixed_full).astype(jnp.bfloat16)
    grad_tokens, gain_first = joint(
        first_map, first_partial, (tokens, grad_middle), norm_gains, (jnp.float32,), 1, False, 4
    )
    mixed_grad = dot_outer(rows_all, mixed_low).astype(jnp.bfloat16)
    gain_columns = jnp.concatenate([gain_first, gain_branch, gain_mid, gain_last], axis=0).T
    head_each = head_width // count
    head_columns = jnp.stack([gain_query, gain_key], axis=1).reshape(count, head_each, 2)
    head_columns = jnp.pad(head_columns, ((0, 0), (0, own_rows - head_each), (0, 0)))
    gain_tile = jnp.concatenate([gain_columns, head_columns.reshape(width, 2)], axis=1)
    gain_tile = jnp.pad(gain_tile, ((0, 0), (0, 128 - gain_tile.shape[1]))).astype(jnp.bfloat16)
    grads = jnp.concatenate([mixed_grad, output_grad, pair_grad, down_grad, gain_tile], axis=1)
    grads = grads.reshape(count, own_rows, -1)
    grads = jnp.pad(grads, ((0, 0), (0, padded_rows - own_rows), (0, 0)))
    kv_each = keyvalue_weight.shape[1] // 4
    split = grads.shape[2] // 256 * 128
    summed, joined = closing(grads, (head_width, kv_each, 128), split, count)
    summed = summed[:own_rows]
    joined = joined[:own_rows]
    me = lax.axis_index("tensor")
    gains_part = lax.dynamic_slice(joined[:, kv_each : kv_each + 4].T, (me, 0), (1, own_rows))
    head_own = head_each // 4
    heads_part = lax.dynamic_slice(joined[:, kv_each + 4 : kv_each + 6].T, (0, me * head_own), (2, head_own))
    middle_at = ends[3] + hidden_width
    return (
        outcome,
        grad_tokens,
        summed[:, : ends[1]],
        joined[:, :kv_each],
        summed[:, ends[2] : ends[3]].T,
        summed[:, ends[3] : middle_at],
        summed[:, middle_at : ends[4]],
        summed[:, ends[4] : ends[5]].T,
        gains_part,
        heads_part,
    )


def solution(mesh):
    placed = (
        P(("dp", "tensor"), None),
        P(("dp", "tensor")),
        P("dp", "tensor"),
        P("dp", None),
        P("tensor", "dp"),
        P("dp", "tensor"),
        P("dp", "tensor"),
        P("tensor", "dp"),
        P(),
        P(),
        P(("dp", "tensor"), None),
    )
    return jax.shard_map(
        body,
        mesh=mesh,
        in_specs=placed,
        out_specs=(
            P(("dp", "tensor"), None),
            P(("dp", "tensor"), None),
            P("dp", "tensor"),
            P("dp", "tensor"),
            P("tensor", "dp"),
            P("dp", "tensor"),
            P("dp", "tensor"),
            P("tensor", "dp"),
            P("tensor", "dp"),
            P(None, ("dp", "tensor")),
        ),
        check_vma=False,
    )
```

```python
import functools

import jax
import jax.numpy as jnp
from jax import lax
from jax.experimental import pallas as pl
from jax.experimental.pallas import tpu as pltpu
from jax.sharding import PartitionSpec as P

epsilon = 1e-06
rope_base = 1000000.0
score_scale = 0.0625
MESH = pl.DeviceIdType.MESH
chunk_count = 4
vmem_bytes = 56 * 2**20
in_vmem = pl.BlockSpec(memory_space=pltpu.VMEM)


def norm_rows(values, scaling):
    return values * lax.rsqrt(jnp.mean(values * values, axis=-1, keepdims=True) + epsilon) * scaling


def norm_pull(values, scaling, grad):
    inverse = lax.rsqrt(jnp.mean(values * values, axis=-1, keepdims=True) + epsilon)
    scaled = grad * scaling
    inner = jnp.mean(values * scaled, axis=-1, keepdims=True)
    pulled = inverse * scaled - values * (inverse * inverse * inverse * inner)
    return pulled, jnp.sum(grad * values * inverse, axis=0, keepdims=True)


def angles(length, head_width):
    halfway = head_width // 2
    places = jnp.arange(length, dtype=jnp.float32)[:, None]
    frequency = rope_base ** (-2.0 * jnp.arange(halfway, dtype=jnp.float32) / head_width)
    phases = places * frequency[None, :]
    return (jnp.cos(phases), jnp.sin(phases))


def rotate(values, cosine_table, sine_table):
    halfway = values.shape[-1] // 2
    leading = values[..., :halfway]
    trailing = values[..., halfway:]
    return jnp.concatenate(
        [
            leading * cosine_table - trailing * sine_table,
            trailing * cosine_table + leading * sine_table,
        ],
        axis=-1,
    )


def activate(gating, upward):
    return jax.nn.gelu(gating, approximate=True) * upward


def dot_rows(left_side, right_side):
    return jnp.dot(left_side, right_side, preferred_element_type=jnp.float32)


def dot_inner(left_side, right_side):
    return lax.dot_general(
        left_side, right_side, (((1,), (1,)), ((), ())), preferred_element_type=jnp.float32
    )


def dot_outer(left_side, right_side):
    return lax.dot_general(
        left_side, right_side, (((0,), (0,)), ((), ())), preferred_element_type=jnp.float32
    )


def send(source, target, send_sem, recv_sem, device):
    return pltpu.make_async_remote_copy(
        src_ref=source,
        dst_ref=target,
        send_sem=send_sem,
        recv_sem=recv_sem,
        device_id=device,
        device_id_type=MESH,
    )


def tensor_peers():
    me = lax.axis_index("tensor")
    chip = me // 2
    core = me % 2
    mate = chip * 2 + 1 - core
    across = (1 - chip) * 2 + core
    diagonal = (1 - chip) * 2 + 1 - core
    return me, mate, across, diagonal


def ring_place(index, count):
    odd = index % 2
    return (index // 2) * (1 - odd) + (count - 1 - index // 2) * odd


def ring_index(place, count):
    back = place // (count // 2)
    return (2 * place) * (1 - back) + (2 * (count - 1 - place) + 1) * back


def greet(targets):
    barrier = pltpu.get_barrier_semaphore()
    for target in targets:
        pl.semaphore_signal(barrier, inc=1, device_id=target, device_id_type=MESH)
    pl.semaphore_wait(barrier, len(targets))


def call(kernel, arguments, outputs, scratch, collective_id):
    return pl.pallas_call(
        kernel,
        out_shape=outputs,
        in_specs=[in_vmem] * len(arguments),
        out_specs=[in_vmem] * len(outputs),
        scratch_shapes=scratch,
        compiler_params=pltpu.CompilerParams(
            collective_id=collective_id, has_side_effects=True, vmem_limit_bytes=vmem_bytes
        ),
    )(*arguments)


class Spread:
    def __init__(self, gathered, send_sems, recv_sems, rows):
        self.gathered, self.send_sems, self.recv_sems, self.rows = gathered, send_sems, recv_sems, rows
        self.me, self.mate, self.across, self.diagonal = tensor_peers()
        self.sent = []

    def copy(self, flow, owner, chunk, device):
        part = self.gathered.at[owner, pl.ds(chunk * self.rows, self.rows)]
        return send(
            part, part, self.send_sems.at[flow, chunk], self.recv_sems.at[flow, chunk], {"tensor": device}
        )

    def give(self, chunk):
        for flow, device in ((0, self.across), (1, self.mate)):
            copy = self.copy(flow, self.me, chunk, device)
            copy.start()
            self.sent.append(copy)

    def forward(self, chunk):
        self.copy(0, self.across, chunk, self.across).wait_recv()
        copy = self.copy(2, self.across, chunk, self.mate)
        copy.start()
        self.sent.append(copy)

    def finish(self, chunks):
        for chunk in range(chunks):
            self.copy(1, self.mate, chunk, self.mate).wait_recv()
            self.copy(2, self.diagonal, chunk, self.mate).wait_recv()
        for copy in self.sent:
            copy.wait_send()


def ring_peers(count):
    place = ring_place(lax.axis_index("dp"), count)
    right = ring_index((place + 1) % count, count)
    left = ring_index((place + count - 1) % count, count)
    return place, right, left


class RingGather:
    def __init__(self, full, send_sems, recv_sems, count):
        self.full, self.send_sems, self.recv_sems, self.count = full, send_sems, recv_sems, count
        self.place, self.right, self.left = ring_peers(count)
        self.last = count // 2 - 1
        self.sent = []

    def copy(self, way, step, owner):
        part = self.full.at[owner]
        if step == self.last:
            half = self.full.shape[2] // 2
            part = self.full.at[owner, :, pl.ds(half * way, half)]
        device = {"dp": self.left if way else self.right}
        return send(part, part, self.send_sems.at[way, step], self.recv_sems.at[way, step], device)

    def owner(self, way, step):
        shift = step if way else self.count - step
        return ring_index((self.place + shift) % self.count, self.count)

    def targets(self):
        return [{"dp": self.right}, {"dp": self.left}]

    def steps(self):
        return range(self.last + 2)

    def advance(self, step):
        for way in (0, 1):
            if step > 0:
                self.copy(way, step - 1, self.owner(way, step)).wait_recv()
            if step <= self.last:
                copy = self.copy(way, step, self.owner(way, step))
                copy.start()
                self.sent.append(copy)

    def finish(self):
        for copy in self.sent:
            copy.wait_send()


class RingReduce:
    def __init__(self, flows, slots, send_sems, recv_sems, count):
        self.flows, self.slots, self.send_sems, self.recv_sems, self.count = flows, slots, send_sems, recv_sems, count
        self.place, self.right, self.left = ring_peers(count)

    def chunk(self, way, step):
        shift = 1 + step if way else 2 * self.count - 1 - step
        return ring_index((self.place + shift) % self.count, self.count)

    def copy(self, flow, step):
        way, grads, start, size = self.flows[flow][:4]
        if step == 0:
            source = grads.at[self.chunk(way, 0), :, pl.ds(start, size)]
        else:
            source = self.slots[flow].at[step - 1]
        device = {"dp": self.left if way else self.right}
        return send(
            source, self.slots[flow].at[step], self.send_sems.at[flow, step], self.recv_sems.at[flow, step], device
        )

    def targets(self):
        return [{"dp": self.right}, {"dp": self.left}]

    def steps(self):
        return range(self.count)

    def advance(self, step):
        for flow, (way, grads, start, size, target, place) in enumerate(self.flows):
            if step == 0:
                self.copy(flow, 0).start()
                continue
            self.copy(flow, step - 1).wait_recv()
            own = grads[self.chunk(way, step), :, pl.ds(start, size)].astype(jnp.float32)
            total = self.slots[flow][step - 1].astype(jnp.float32) + own
            if step < self.count - 1:
                self.slots[flow][step - 1] = total.astype(jnp.bfloat16)
                self.copy(flow, step).start()
            else:
                target[:, pl.ds(place, size)] = total

    def finish(self):
        for step in range(self.count - 1):
            for flow in range(len(self.flows)):
                self.copy(flow, step).wait_send()


def reduce_scratch(flow_sizes, rows, count):
    slots = [pltpu.VMEM((count - 1, rows, size), jnp.bfloat16) for size in flow_sizes]
    return slots + [pltpu.SemaphoreType.DMA((len(flow_sizes), count - 1))] * 2


def gather_scratch(count):
    return [pltpu.SemaphoreType.DMA((2, count // 2))] * 2


def place_shard(full, weights, mine):
    start = 0
    for weight in weights:
        full[mine, pl.ds(0, weight.shape[0]), pl.ds(start, weight.shape[1])] = weight[...]
        start += weight.shape[1]


def gathered_shape(weights, padded_rows, count):
    columns = sum(weight.shape[1] for weight in weights)
    return jax.ShapeDtypeStruct((count, padded_rows, columns), jnp.bfloat16)


def opening_kernel(
    count, tokens, segments, gains, first, second, third, rows_all, segment_all, full, send_sems, recv_sems, seg_send, seg_recv, ring_send, ring_recv
):
    me, mate, across, diagonal = tensor_peers()
    ring = RingGather(full, ring_send, ring_recv, count)
    greet([{"tensor": mate}, {"tensor": across}, {"tensor": diagonal}, {"dp": ring.right}, {"dp": ring.left}])
    place_shard(full, (first, second, third), lax.axis_index("dp"))
    ring.advance(0)
    segment_all[me] = segments[...]
    spread = Spread(rows_all, send_sems, recv_sems, tokens.shape[0] // chunk_count)
    for chunk in range(chunk_count):
        rows = pl.ds(chunk * spread.rows, spread.rows)
        normed = norm_rows(tokens[rows, :].astype(jnp.float32), gains[0:1, :])
        rows_all[me, rows, :] = normed.astype(jnp.bfloat16)
        spread.give(chunk)
    seg_sent = []
    for flow, device in enumerate((mate, across, diagonal)):
        part = segment_all.at[me]
        copy = send(part, part, seg_send.at[flow], seg_recv.at[flow], {"tensor": device})
        copy.start()
        seg_sent.append(copy)
    ring.advance(1)
    for chunk in range(chunk_count):
        spread.forward(chunk)
    for step in ring.steps()[2:]:
        ring.advance(step)
    spread.finish(chunk_count)
    for flow, device in enumerate((mate, across, diagonal)):
        part = segment_all.at[device]
        send(part, part, seg_send.at[flow], seg_recv.at[flow], {"tensor": device}).wait_recv()
    for copy in seg_sent:
        copy.wait_send()
    ring.finish()


def opening(tokens, segments, gains, weights, padded_rows, count):
    rows, width = tokens.shape
    return call(
        functools.partial(opening_kernel, count),
        (tokens, segments, gains) + weights,
        [
            jax.ShapeDtypeStruct((4, rows, width), jnp.bfloat16),
            jax.ShapeDtypeStruct((4,) + segments.shape, jnp.int32),
            gathered_shape(weights, padded_rows, count),
        ],
        [
            pltpu.SemaphoreType.DMA((3, chunk_count)),
            pltpu.SemaphoreType.DMA((3, chunk_count)),
            pltpu.SemaphoreType.DMA((3,)),
            pltpu.SemaphoreType.DMA((3,)),
        ]
        + gather_scratch(count),
        0,
    )


class IdleRider:
    pace, arrays, inputs, outputs, shapes, scratch = 1, (), 0, 0, [], []

    def __init__(self, count):
        self.count = count

    def build(self, inputs, outputs, scratch, count):
        return self

    def steps(self):
        return ()

    def targets(self):
        return []

    def prepare(self, inputs, outputs):
        pass

    def finish(self):
        pass


class GatherRider:
    pace = 2

    def __init__(self, weights, padded_rows, count):
        self.arrays, self.inputs, self.outputs = weights, len(weights), 1
        self.shapes = [gathered_shape(weights, padded_rows, count)]
        self.scratch = gather_scratch(count)

    def build(self, inputs, outputs, scratch, count):
        return RingGather(outputs[0], scratch[0], scratch[1], count)

    def prepare(self, inputs, outputs):
        place_shard(outputs[0], inputs, lax.axis_index("dp"))


class ReduceRider:
    pace = 1

    def __init__(self, grads, plan, out_columns, count):
        rows = grads[0].shape[1]
        self.arrays, self.inputs, self.outputs, self.plan = grads, len(grads), len(out_columns), plan
        self.shapes = [jax.ShapeDtypeStruct((rows, columns), jnp.float32) for columns in out_columns]
        self.scratch = reduce_scratch([flow[3] for flow in plan], rows, count)

    def build(self, inputs, outputs, scratch, count):
        flows = [(way, inputs[a], start, size, outputs[o], at) for way, a, start, size, o, at in self.plan]
        number = len(flows)
        return RingReduce(flows, scratch[:number], scratch[number], scratch[number + 1], count)

    def prepare(self, inputs, outputs):
        pass


def joint_kernel(row_map, extra_count, row_count, sum_count, spreads, rider, count, *refs):
    refs = list(refs)

    def take(number):
        taken = refs[:number]
        del refs[:number]
        return taken

    (partial,) = take(1)
    extras = take(extra_count)
    (gains,) = take(1)
    rider_in = take(rider.inputs)
    gathered = take(1)[0] if spreads else None
    row_outs = take(row_count)
    sum_outs = take(sum_count)
    rider_out = take(rider.outputs)
    near, outgoing, far, send_sems, recv_sems = take(5)
    if spreads:
        spread_send, spread_recv = take(2)
    ring = rider.build(rider_in, rider_out, refs, count)
    me, mate, across, diagonal = tensor_peers()
    rows_each = partial.shape[1] // chunk_count
    greet([{"tensor": mate}, {"tensor": across}] + ring.targets())
    ring_steps = list(ring.steps())

    def ride():
        if ring_steps:
            ring.advance(ring_steps.pop(0))


    def near_copy(flow, chunk):
        owner = mate if flow else diagonal
        part = pl.ds(chunk * rows_each, rows_each)
        return send(
            partial.at[owner, part], near.at[flow, part], send_sems.at[flow, chunk], recv_sems.at[flow, chunk], {"tensor": mate}
        )

    def far_copy(chunk):
        part = pl.ds(chunk * rows_each, rows_each)
        return send(outgoing.at[part], far.at[part], send_sems.at[2, chunk], recv_sems.at[2, chunk], {"tensor": across})

    for flow in (0, 1):
        for chunk in range(chunk_count):
            near_copy(flow, chunk).start()
    rider.prepare(rider_in, rider_out)
    ride()
    for chunk in range(chunk_count):
        part = pl.ds(chunk * rows_each, rows_each)
        near_copy(0, chunk).wait_recv()
        total = partial[across, part, :].astype(jnp.float32) + near[0, part, :].astype(jnp.float32)
        outgoing[part, :] = total.astype(jnp.bfloat16)
        far_copy(chunk).start()
    ride()
    if spreads:
        spread = Spread(gathered, spread_send, spread_recv, rows_each)
    sums = None
    for chunk in range(chunk_count):
        part = pl.ds(chunk * rows_each, rows_each)
        near_copy(1, chunk).wait_recv()
        total = partial[me, part, :].astype(jnp.float32) + near[1, part, :].astype(jnp.float32)
        far_copy(chunk).wait_recv()
        total = total + far[part, :].astype(jnp.float32)
        given, rows_out, sums_out = row_map(total, [extra[part, :] for extra in extras], gains)
        if spreads:
            gathered[me, part, :] = given.astype(jnp.bfloat16)
            spread.give(chunk)
        for ref, value in zip(row_outs, rows_out):
            ref[part, :] = value.astype(ref.dtype)
        sums = sums_out if sums is None else [held + new for held, new in zip(sums, sums_out)]
        if spreads and chunk > 0:
            spread.forward(chunk - 1)
        if chunk % rider.pace == rider.pace - 1:
            ride()
    for ref, value in zip(sum_outs, sums):
        ref[...] = value
    if spreads:
        spread.forward(chunk_count - 1)
    while ring_steps:
        ride()
    if spreads:
        spread.finish(chunk_count)
    for chunk in range(chunk_count):
        near_copy(0, chunk).wait_send()
        near_copy(1, chunk).wait_send()
        far_copy(chunk).wait_send()
    ring.finish()


def joint(row_map, partial, extras, gains, row_types, sum_count, spreads, rider, count, collective_id):
    rows, width = partial.shape[0] // 4, partial.shape[1]
    outputs = []
    if spreads:
        outputs.append(jax.ShapeDtypeStruct((4, rows, width), jnp.bfloat16))
    outputs += [jax.ShapeDtypeStruct((rows, width), kind) for kind in row_types]
    outputs += [jax.ShapeDtypeStruct((1, width), jnp.float32)] * sum_count
    outputs += rider.shapes
    scratch = [
        pltpu.VMEM((2, rows, width), jnp.bfloat16),
        pltpu.VMEM((rows, width), jnp.bfloat16),
        pltpu.VMEM((rows, width), jnp.bfloat16),
        pltpu.SemaphoreType.DMA((3, chunk_count)),
        pltpu.SemaphoreType.DMA((3, chunk_count)),
    ]
    if spreads:
        scratch += [pltpu.SemaphoreType.DMA((3, chunk_count))] * 2
    scratch += rider.scratch
    found = list(call(
        functools.partial(joint_kernel, row_map, len(extras), len(row_types), sum_count, spreads, rider, count),
        (partial.reshape(4, rows, width),) + tuple(extras) + (gains,) + tuple(rider.arrays),
        outputs,
        scratch,
        collective_id,
    ))
    if spreads:
        found[0] = found[0].reshape(4 * rows, width)
    return found


def branch_map(branch, extras, gains):
    middle = extras[0].astype(jnp.float32) + norm_rows(branch, gains[1:2, :])
    return norm_rows(middle, gains[2:3, :]), [branch, middle], []


def ffn_map(ffn_out, extras, gains):
    middle, cotangent = extras
    outcome = middle + norm_rows(ffn_out, gains[3:4, :])
    grad_ffn, gain_last = norm_pull(ffn_out, gains[3:4, :], cotangent.astype(jnp.float32))
    return grad_ffn, [outcome], [gain_last]


def middle_map(grad_mid_normed, extras, gains):
    middle, branch, cotangent = extras
    pulled, gain_mid = norm_pull(middle, gains[2:3, :], grad_mid_normed)
    grad_middle = cotangent.astype(jnp.float32) + pulled
    grad_branch, gain_branch = norm_pull(branch, gains[1:2, :], grad_middle)
    return grad_branch, [grad_middle], [gain_branch, gain_mid]


def first_map(grad_first_normed, extras, gains):
    tokens, grad_middle = extras
    pulled, gain_first = norm_pull(tokens.astype(jnp.float32), gains[0:1, :], grad_first_normed)
    return None, [grad_middle + pulled], [gain_first]


def closing_kernel(count, each, mixed, gain_tile, query_sum, joined, kv_sum, gain_sum, staged, arrived, tail_send, tail_recv, *ring_refs):
    me = lax.axis_index("tensor")
    others = [(me + shift) % 4 for shift in (1, 2, 3)]
    first = query_sum.shape[1]
    half = kv_sum.shape[1] // 2
    tail = gain_sum.shape[1]
    flows = [
        (1, mixed, first, half, kv_sum, 0),
        (0, mixed, 0, first, query_sum, 0),
        (1, mixed, first + half, half, kv_sum, half),
        (0, gain_tile, 0, tail, gain_sum, 0),
    ]
    ring = RingReduce(flows, ring_refs[:4], ring_refs[4], ring_refs[5], count)
    greet([{"dp": ring.right}, {"dp": ring.left}] + [{"tensor": other} for other in others])
    for step in ring.steps():
        ring.advance(step)
    for device in range(4):
        staged[device, :, pl.ds(0, each)] = kv_sum[:, pl.ds(each * device, each)]
        staged[device, :, pl.ds(each, tail)] = gain_sum[...]
    tails = []
    for slot, other in enumerate(others):
        copy = send(staged.at[other], arrived.at[slot], tail_send.at[slot], tail_recv.at[slot], {"tensor": other})
        copy.start()
        tails.append(copy)
    total = staged[me]
    for slot in range(3):
        tails[slot].wait_recv()
        total = total + arrived[slot]
    joined[...] = total
    for copy in tails:
        copy.wait_send()
    ring.finish()


def closing(mixed, gain_tile, query_columns, count):
    rows, width = mixed.shape[1:]
    tail = gain_tile.shape[2]
    kv_columns = width - query_columns
    each = kv_columns // 4
    return call(
        functools.partial(closing_kernel, count, each),
        (mixed, gain_tile),
        [
            jax.ShapeDtypeStruct((rows, query_columns), jnp.float32),
            jax.ShapeDtypeStruct((rows, each + tail), jnp.float32),
        ],
        [
            pltpu.VMEM((rows, kv_columns), jnp.float32),
            pltpu.VMEM((rows, tail), jnp.float32),
            pltpu.VMEM((4, rows, each + tail), jnp.float32),
            pltpu.VMEM((3, rows, each + tail), jnp.float32),
            pltpu.SemaphoreType.DMA((3,)),
            pltpu.SemaphoreType.DMA((3,)),
        ]
        + reduce_scratch([kv_columns // 2, query_columns, kv_columns // 2, tail], rows, count),
        5,
    )


def body(
    tokens,
    segments,
    query_weight,
    keyvalue_weight,
    output_weight,
    gate_weight,
    up_weight,
    down_weight,
    norm_gains,
    headnorm_gains,
    cotangent,
):
    head_width = headnorm_gains.shape[1]
    width = tokens.shape[1]
    hidden_width = gate_weight.shape[1]
    count = lax.axis_size("dp")
    own_rows = query_weight.shape[0]
    padded_rows = -(-own_rows // 16) * 16
    seg_tile = segments.reshape(-1, 128)
    rows_all, segment_all, full = opening(
        tokens, seg_tile, norm_gains, (query_weight, keyvalue_weight, output_weight.T), padded_rows, count
    )
    rows_all = rows_all.reshape(-1, width)
    segment_all = segment_all.reshape(-1)

    def join_blocks(blocks):
        return blocks[:, :own_rows].reshape(width, -1)

    def cut_blocks(whole):
        blocks = whole.astype(jnp.bfloat16).reshape(count, own_rows, -1)
        return jnp.pad(blocks, ((0, 0), (0, padded_rows - own_rows), (0, 0)))

    full = join_blocks(full)
    mixed_full = full[:, : 3 * head_width]
    output_full = full[:, 3 * head_width :]
    length = rows_all.shape[0]
    block_rows = min(512, length)
    cosine_table, sine_table = angles(length, head_width)

    def query_map(raw_values, scaling):
        return rotate(norm_rows(raw_values, scaling), cosine_table, sine_table) * score_scale

    def key_map(raw_values, scaling):
        return rotate(norm_rows(raw_values, scaling), cosine_table, sine_table)

    mixed_raw = dot_rows(rows_all, mixed_full)
    query_raw = mixed_raw[:, :head_width]
    keyvalue_raw = mixed_raw[:, head_width:]
    query_rows = query_map(query_raw, headnorm_gains[0]).astype(jnp.bfloat16)
    key_rows = key_map(keyvalue_raw[:, :head_width], headnorm_gains[1]).astype(jnp.bfloat16)
    value_rows = keyvalue_raw[:, head_width:].astype(jnp.bfloat16)

    def masked_scores(row_from, row_to):
        scores = dot_inner(query_rows[row_from:row_to], key_rows[:row_to])
        row_places = row_from + jnp.arange(row_to - row_from)
        key_places = jnp.arange(row_to)
        allowed = (key_places[None, :] <= row_places[:, None]) & (
            segment_all[row_from:row_to][:, None] == segment_all[:row_to][None, :]
        )
        return jnp.where(allowed, scores, -jnp.inf)

    pieces_out = []
    pieces_total = []
    for block_id in range(length // block_rows):
        row_from = block_id * block_rows
        row_to = row_from + block_rows
        scores = masked_scores(row_from, row_to)
        row_peak = jnp.max(scores, axis=-1, keepdims=True)
        raised = jnp.exp(scores - row_peak)
        row_total = jnp.sum(raised, axis=-1, keepdims=True)
        weights_low = (raised / row_total).astype(jnp.bfloat16)
        pieces_out.append(dot_rows(weights_low, value_rows[:row_to]).astype(jnp.bfloat16))
        pieces_total.append(row_peak + jnp.log(row_total))
    attended = jnp.concatenate(pieces_out, axis=0)
    log_totals = jnp.concatenate(pieces_total, axis=0)
    branch_partial = dot_inner(attended, output_full).astype(jnp.bfloat16)
    carried = GatherRider((gate_weight, up_weight, down_weight.T), padded_rows, count)
    mid_all, branch, middle, full = joint(
        branch_map, branch_partial, (tokens,), norm_gains, (jnp.float32, jnp.float32), 0, True, carried, count, 1
    )
    full = join_blocks(full)
    pair_full = full[:, : 2 * hidden_width]
    down_full = full[:, 2 * hidden_width :]
    paired = dot_rows(mid_all, pair_full)
    gating = paired[:, :hidden_width]
    upward = paired[:, hidden_width:]
    idle = IdleRider(count)
    hidden = activate(gating, upward).astype(jnp.bfloat16)
    ffn_partial = dot_inner(hidden, down_full).astype(jnp.bfloat16)
    grad_ffn_all, outcome, gain_last = joint(
        ffn_map, ffn_partial, (middle, cotangent), norm_gains, (jnp.bfloat16,), 1, True, idle, count, 2
    )
    grad_hidden = dot_rows(grad_ffn_all, down_full)
    down_grad = cut_blocks(dot_outer(grad_ffn_all, hidden))
    ignored, pull_active = jax.vjp(activate, gating, upward)
    grad_gating, grad_upward = pull_active(grad_hidden)
    paired_low = jnp.concatenate(
        [grad_gating.astype(jnp.bfloat16), grad_upward.astype(jnp.bfloat16)], axis=1
    )
    mid_partial = dot_inner(paired_low, pair_full).astype(jnp.bfloat16)
    pair_grad = cut_blocks(dot_outer(mid_all, paired_low))
    down_half = hidden_width // 2
    plan = (
        (0, 0, 0, hidden_width, 0, 0),
        (1, 0, hidden_width, hidden_width, 1, 0),
        (0, 1, 0, down_half, 2, 0),
        (1, 1, down_half, down_half, 2, down_half),
    )
    carried = ReduceRider((pair_grad, down_grad), plan, (hidden_width,) * 3, count)
    branch_all, grad_middle, gain_branch, gain_mid, gate_part, up_part, down_part = joint(
        middle_map, mid_partial, (middle, branch, cotangent), norm_gains, (jnp.float32,), 2, True, carried, count, 3
    )
    output_grad = cut_blocks(dot_outer(branch_all, attended))
    grad_attended = dot_rows(branch_all, output_full).astype(jnp.bfloat16)
    grad_query_parts = []
    grad_keys = jnp.zeros((length, head_width), jnp.float32)
    grad_values = jnp.zeros((length, head_width), jnp.float32)
    for block_id in range(length // block_rows):
        row_from = block_id * block_rows
        row_to = row_from + block_rows
        scores = masked_scores(row_from, row_to)
        weights_full = jnp.exp(scores - log_totals[row_from:row_to])
        weights_low = weights_full.astype(jnp.bfloat16)
        grad_block = grad_attended[row_from:row_to]
        grad_weights = dot_inner(grad_block, value_rows[:row_to])
        row_inner = jnp.sum(weights_full * grad_weights, axis=-1, keepdims=True)
        grad_scores = (weights_full * (grad_weights - row_inner)).astype(jnp.bfloat16)
        grad_query_parts.append(dot_rows(grad_scores, key_rows[:row_to]))
        grad_keys = grad_keys.at[:row_to].add(dot_outer(grad_scores, query_rows[row_from:row_to]))
        grad_values = grad_values.at[:row_to].add(dot_outer(weights_low, grad_block))
    grad_query = jnp.concatenate(grad_query_parts, axis=0)
    ignored, pull_query = jax.vjp(query_map, query_raw, headnorm_gains[0])
    grad_query_raw, gain_query = pull_query(grad_query)
    ignored, pull_key = jax.vjp(key_map, keyvalue_raw[:, :head_width], headnorm_gains[1])
    grad_key_raw, gain_key = pull_key(grad_keys)
    mixed_low = jnp.concatenate([grad_query_raw, grad_key_raw, grad_values], axis=1).astype(jnp.bfloat16)
    first_partial = dot_inner(mixed_low, mixed_full).astype(jnp.bfloat16)
    half = head_width // 2
    plan = ((0, 0, 0, half, 0, 0), (1, 0, half, half, 0, half))
    carried = ReduceRider((output_grad,), plan, (head_width,), count)
    grad_tokens, gain_first, output_part = joint(
        first_map, first_partial, (tokens, grad_middle), norm_gains, (jnp.float32,), 1, False, carried, count, 4
    )
    mixed_grad = cut_blocks(dot_outer(rows_all, mixed_low))
    gain_columns = jnp.concatenate([gain_first, gain_branch, gain_mid, gain_last], axis=0).T
    head_each = head_width // count
    head_columns = jnp.stack([gain_query, gain_key], axis=1).reshape(count, head_each, 2)
    head_columns = jnp.pad(head_columns, ((0, 0), (0, own_rows - head_each), (0, 0)))
    gain_tile = jnp.concatenate([gain_columns, head_columns.reshape(width, 2)], axis=1)
    gain_tile = cut_blocks(jnp.pad(gain_tile, ((0, 0), (0, 128 - gain_tile.shape[1]))))
    kv_each = keyvalue_weight.shape[1] // 4
    query_part, joined = closing(mixed_grad, gain_tile, head_width, count)
    joined = joined[:own_rows]
    me = lax.axis_index("tensor")
    gains_part = lax.dynamic_slice(joined[:, kv_each : kv_each + 4].T, (me, 0), (1, own_rows))
    head_own = head_each // 4
    heads_part = lax.dynamic_slice(joined[:, kv_each + 4 : kv_each + 6].T, (0, me * head_own), (2, head_own))
    return (
        outcome,
        grad_tokens,
        query_part[:own_rows],
        joined[:, :kv_each],
        output_part[:own_rows].T,
        gate_part[:own_rows],
        up_part[:own_rows],
        down_part[:own_rows].T,
        gains_part,
        heads_part,
    )


def solution(mesh):
    placed = (
        P(("dp", "tensor"), None),
        P(("dp", "tensor")),
        P("dp", "tensor"),
        P("dp", None),
        P("tensor", "dp"),
        P("dp", "tensor"),
        P("dp", "tensor"),
        P("tensor", "dp"),
        P(),
        P(),
        P(("dp", "tensor"), None),
    )
    return jax.shard_map(
        body,
        mesh=mesh,
        in_specs=placed,
        out_specs=(
            P(("dp", "tensor"), None),
            P(("dp", "tensor"), None),
            P("dp", "tensor"),
            P("dp", "tensor"),
            P("tensor", "dp"),
            P("dp", "tensor"),
            P("dp", "tensor"),
            P("tensor", "dp"),
            P("tensor", "dp"),
            P(None, ("dp", "tensor")),
        ),
        check_vma=False,
    )
```

```python
import functools

import jax
import jax.numpy as jnp
from jax import lax
from jax.experimental import pallas as pl
from jax.experimental.pallas import tpu as pltpu
from jax.sharding import PartitionSpec as P

epsilon = 1e-06
rope_base = 1000000.0
score_scale = 0.0625
MESH = pl.DeviceIdType.MESH
chunk_count = 4
vmem_bytes = 56 * 2**20
in_vmem = pl.BlockSpec(memory_space=pltpu.VMEM)


def norm_rows(values, scaling):
    return values * lax.rsqrt(jnp.mean(values * values, axis=-1, keepdims=True) + epsilon) * scaling


def norm_pull(values, scaling, grad):
    inverse = lax.rsqrt(jnp.mean(values * values, axis=-1, keepdims=True) + epsilon)
    scaled = grad * scaling
    inner = jnp.mean(values * scaled, axis=-1, keepdims=True)
    pulled = inverse * scaled - values * (inverse * inverse * inverse * inner)
    return pulled, jnp.sum(grad * values * inverse, axis=0, keepdims=True)


def angles(length, head_width):
    halfway = head_width // 2
    places = jnp.arange(length, dtype=jnp.float32)[:, None]
    frequency = rope_base ** (-2.0 * jnp.arange(halfway, dtype=jnp.float32) / head_width)
    phases = places * frequency[None, :]
    return (jnp.cos(phases), jnp.sin(phases))


def rotate(values, cosine_table, sine_table):
    halfway = values.shape[-1] // 2
    leading = values[..., :halfway]
    trailing = values[..., halfway:]
    return jnp.concatenate(
        [
            leading * cosine_table - trailing * sine_table,
            trailing * cosine_table + leading * sine_table,
        ],
        axis=-1,
    )


def activate(gating, upward):
    return jax.nn.gelu(gating, approximate=True) * upward


def dot_rows(left_side, right_side):
    return jnp.dot(left_side, right_side, preferred_element_type=jnp.float32)


def dot_inner(left_side, right_side):
    return lax.dot_general(
        left_side, right_side, (((1,), (1,)), ((), ())), preferred_element_type=jnp.float32
    )


def dot_outer(left_side, right_side):
    return lax.dot_general(
        left_side, right_side, (((0,), (0,)), ((), ())), preferred_element_type=jnp.float32
    )


def send(source, target, send_sem, recv_sem, device):
    return pltpu.make_async_remote_copy(
        src_ref=source,
        dst_ref=target,
        send_sem=send_sem,
        recv_sem=recv_sem,
        device_id=device,
        device_id_type=MESH,
    )


def tensor_peers():
    me = lax.axis_index("tensor")
    chip = me // 2
    core = me % 2
    mate = chip * 2 + 1 - core
    across = (1 - chip) * 2 + core
    diagonal = (1 - chip) * 2 + 1 - core
    return me, mate, across, diagonal


def ring_place(index, count):
    odd = index % 2
    return (index // 2) * (1 - odd) + (count - 1 - index // 2) * odd


def ring_index(place, count):
    back = place // (count // 2)
    return (2 * place) * (1 - back) + (2 * (count - 1 - place) + 1) * back


def greet(targets):
    barrier = pltpu.get_barrier_semaphore()
    for target in targets:
        pl.semaphore_signal(barrier, inc=1, device_id=target, device_id_type=MESH)
    pl.semaphore_wait(barrier, len(targets))


def call(kernel, arguments, outputs, scratch, collective_id):
    return pl.pallas_call(
        kernel,
        out_shape=outputs,
        in_specs=[in_vmem] * len(arguments),
        out_specs=[in_vmem] * len(outputs),
        scratch_shapes=scratch,
        compiler_params=pltpu.CompilerParams(
            collective_id=collective_id, has_side_effects=True, vmem_limit_bytes=vmem_bytes
        ),
    )(*arguments)


class Spread:
    def __init__(self, gathered, send_sems, recv_sems, rows):
        self.gathered, self.send_sems, self.recv_sems, self.rows = gathered, send_sems, recv_sems, rows
        self.me, self.mate, self.across, self.diagonal = tensor_peers()
        self.sent = []

    def copy(self, flow, owner, chunk, device):
        part = self.gathered.at[owner, pl.ds(chunk * self.rows, self.rows)]
        return send(
            part, part, self.send_sems.at[flow, chunk], self.recv_sems.at[flow, chunk], {"tensor": device}
        )

    def give(self, chunk):
        for flow, device in ((0, self.across), (1, self.mate)):
            copy = self.copy(flow, self.me, chunk, device)
            copy.start()
            self.sent.append(copy)

    def forward(self, chunk):
        self.copy(0, self.across, chunk, self.across).wait_recv()
        copy = self.copy(2, self.across, chunk, self.mate)
        copy.start()
        self.sent.append(copy)

    def finish(self, chunks):
        for chunk in range(chunks):
            self.copy(1, self.mate, chunk, self.mate).wait_recv()
            self.copy(2, self.diagonal, chunk, self.mate).wait_recv()
        for copy in self.sent:
            copy.wait_send()


def ring_peers(count):
    place = ring_place(lax.axis_index("dp"), count)
    right = ring_index((place + 1) % count, count)
    left = ring_index((place + count - 1) % count, count)
    return place, right, left


class RingGather:
    def __init__(self, full, send_sems, recv_sems, count):
        self.full, self.send_sems, self.recv_sems, self.count = full, send_sems, recv_sems, count
        self.place, self.right, self.left = ring_peers(count)
        self.last = count // 2 - 1
        self.sent = []

    def copy(self, way, step, owner):
        part = self.full.at[owner]
        if step == self.last:
            half = self.full.shape[2] // 2
            part = self.full.at[owner, :, pl.ds(half * way, half)]
        device = {"dp": self.left if way else self.right}
        return send(part, part, self.send_sems.at[way, step], self.recv_sems.at[way, step], device)

    def owner(self, way, step):
        shift = step if way else self.count - step
        return ring_index((self.place + shift) % self.count, self.count)

    def targets(self):
        return [{"dp": self.right}, {"dp": self.left}]

    def steps(self):
        return range(self.last + 2)

    def advance(self, step):
        for way in (0, 1):
            if step > 0:
                self.copy(way, step - 1, self.owner(way, step)).wait_recv()
            if step <= self.last:
                copy = self.copy(way, step, self.owner(way, step))
                copy.start()
                self.sent.append(copy)

    def finish(self):
        for copy in self.sent:
            copy.wait_send()


class RingReduce:
    def __init__(self, flows, slots, send_sems, recv_sems, count):
        self.flows, self.slots, self.send_sems, self.recv_sems, self.count = flows, slots, send_sems, recv_sems, count
        self.place, self.right, self.left = ring_peers(count)

    def chunk(self, way, step):
        shift = 1 + step if way else 2 * self.count - 1 - step
        return ring_index((self.place + shift) % self.count, self.count)

    def copy(self, flow, step):
        way, grads, start, size = self.flows[flow][:4]
        if step == 0:
            source = grads.at[self.chunk(way, 0), :, pl.ds(start, size)]
        else:
            source = self.slots[flow].at[step - 1]
        device = {"dp": self.left if way else self.right}
        return send(
            source, self.slots[flow].at[step], self.send_sems.at[flow, step], self.recv_sems.at[flow, step], device
        )

    def targets(self):
        return [{"dp": self.right}, {"dp": self.left}]

    def steps(self):
        return range(self.count)

    def advance(self, step):
        for flow, (way, grads, start, size, target, place) in enumerate(self.flows):
            if step == 0:
                self.copy(flow, 0).start()
                continue
            self.copy(flow, step - 1).wait_recv()
            own = grads[self.chunk(way, step), :, pl.ds(start, size)].astype(jnp.float32)
            total = self.slots[flow][step - 1].astype(jnp.float32) + own
            if step < self.count - 1:
                self.slots[flow][step - 1] = total.astype(jnp.bfloat16)
                self.copy(flow, step).start()
            else:
                target[:, pl.ds(place, size)] = total

    def finish(self):
        for step in range(self.count - 1):
            for flow in range(len(self.flows)):
                self.copy(flow, step).wait_send()


def reduce_scratch(flow_sizes, rows, count):
    slots = [pltpu.VMEM((count - 1, rows, size), jnp.bfloat16) for size in flow_sizes]
    return slots + [pltpu.SemaphoreType.DMA((len(flow_sizes), count - 1))] * 2


def gather_scratch(count):
    return [pltpu.SemaphoreType.DMA((2, count // 2))] * 2


def place_shard(full, weights, mine):
    start = 0
    for weight in weights:
        full[mine, pl.ds(0, weight.shape[0]), pl.ds(start, weight.shape[1])] = weight[...]
        start += weight.shape[1]


def gathered_shape(weights, padded_rows, count):
    columns = sum(weight.shape[1] for weight in weights)
    return jax.ShapeDtypeStruct((count, padded_rows, columns), jnp.bfloat16)


def opening_kernel(
    count, tokens, segments, gains, first, second, third, rows_all, segment_all, full, send_sems, recv_sems, seg_send, seg_recv, ring_send, ring_recv
):
    me, mate, across, diagonal = tensor_peers()
    ring = RingGather(full, ring_send, ring_recv, count)
    greet([{"tensor": mate}, {"tensor": across}, {"tensor": diagonal}, {"dp": ring.right}, {"dp": ring.left}])
    place_shard(full, (first, second, third), lax.axis_index("dp"))
    ring.advance(0)
    segment_all[me] = segments[...]
    spread = Spread(rows_all, send_sems, recv_sems, tokens.shape[0] // chunk_count)
    for chunk in range(chunk_count):
        rows = pl.ds(chunk * spread.rows, spread.rows)
        normed = norm_rows(tokens[rows, :].astype(jnp.float32), gains[0:1, :])
        rows_all[me, rows, :] = normed.astype(jnp.bfloat16)
        spread.give(chunk)
    seg_sent = []
    for flow, device in enumerate((mate, across, diagonal)):
        part = segment_all.at[me]
        copy = send(part, part, seg_send.at[flow], seg_recv.at[flow], {"tensor": device})
        copy.start()
        seg_sent.append(copy)
    ring.advance(1)
    for chunk in range(chunk_count):
        spread.forward(chunk)
    for step in ring.steps()[2:]:
        ring.advance(step)
    spread.finish(chunk_count)
    for flow, device in enumerate((mate, across, diagonal)):
        part = segment_all.at[device]
        send(part, part, seg_send.at[flow], seg_recv.at[flow], {"tensor": device}).wait_recv()
    for copy in seg_sent:
        copy.wait_send()
    ring.finish()


def opening(tokens, segments, gains, weights, padded_rows, count):
    rows, width = tokens.shape
    return call(
        functools.partial(opening_kernel, count),
        (tokens, segments, gains) + weights,
        [
            jax.ShapeDtypeStruct((4, rows, width), jnp.bfloat16),
            jax.ShapeDtypeStruct((4,) + segments.shape, jnp.int32),
            gathered_shape(weights, padded_rows, count),
        ],
        [
            pltpu.SemaphoreType.DMA((3, chunk_count)),
            pltpu.SemaphoreType.DMA((3, chunk_count)),
            pltpu.SemaphoreType.DMA((3,)),
            pltpu.SemaphoreType.DMA((3,)),
        ]
        + gather_scratch(count),
        0,
    )


class IdleRider:
    pace, arrays, inputs, outputs, shapes, scratch = 1, (), 0, 0, [], []

    def __init__(self, count):
        self.count = count

    def build(self, inputs, outputs, scratch, count):
        return self

    def steps(self):
        return ()

    def targets(self):
        return []

    def prepare(self, inputs, outputs):
        pass

    def finish(self):
        pass


class GatherRider:
    pace = 2

    def __init__(self, weights, padded_rows, count):
        self.arrays, self.inputs, self.outputs = weights, len(weights), 1
        self.shapes = [gathered_shape(weights, padded_rows, count)]
        self.scratch = gather_scratch(count)

    def build(self, inputs, outputs, scratch, count):
        return RingGather(outputs[0], scratch[0], scratch[1], count)

    def prepare(self, inputs, outputs):
        place_shard(outputs[0], inputs, lax.axis_index("dp"))


class ReduceRider:
    pace = 1

    def __init__(self, grads, plan, out_columns, count):
        rows = grads[0].shape[1]
        self.arrays, self.inputs, self.outputs, self.plan = grads, len(grads), len(out_columns), plan
        self.shapes = [jax.ShapeDtypeStruct((rows, columns), jnp.float32) for columns in out_columns]
        self.scratch = reduce_scratch([flow[3] for flow in plan], rows, count)

    def build(self, inputs, outputs, scratch, count):
        flows = [(way, inputs[a], start, size, outputs[o], at) for way, a, start, size, o, at in self.plan]
        number = len(flows)
        return RingReduce(flows, scratch[:number], scratch[number], scratch[number + 1], count)

    def prepare(self, inputs, outputs):
        pass


class FinalExchange:
    def __init__(self, inputs, outputs, scratch, count):
        self.grads, self.gain_rows = inputs[:2], inputs[2]
        self.query_part, self.kv_part, self.output_part, self.gain_sum = outputs
        self.got, self.outgoing, self.far = scratch[0:2], scratch[2:4], scratch[4:6]
        self.mixed_sum, self.staged, self.arrived = scratch[6:9]
        self.gain_tile, self.gain_near, self.gain_mid, self.gain_far = scratch[9:13]
        self.near_sems, self.far_sems, self.kv_sems, self.tile_sems, self.mid_sems = [
            scratch[at : at + 2] for at in range(13, 23, 2)
        ]
        self.count, self.half = count, count // 2
        self.mine = lax.axis_index("dp")
        self.row, self.parity = self.mine // 2, self.mine % 2
        self.partner = self.row * 2 + 1 - self.parity
        self.me = lax.axis_index("tensor")
        self.others = [(self.me + shift) % 4 for shift in (1, 2, 3)]
        self.peers = [(self.mine + shift) % count for shift in range(1, count)]
        self.sent = []

    def targets(self):
        return [{"dp": peer} for peer in self.peers] + [{"tensor": tensor_peers()[3]}]

    def steps(self):
        return range(10)

    def begin(self, copy):
        copy.start()
        self.sent.append(copy)

    def near_copy(self, array, block):
        return send(
            self.grads[array].at[2 * block + 1 - self.parity],
            self.got[array].at[block],
            self.near_sems[0].at[array, block],
            self.near_sems[1].at[array, block],
            {"dp": self.partner},
        )

    def far_copy(self, array, shift):
        device = 2 * ((self.row + shift) % self.half) + self.parity
        slot = shift - 1
        return send(
            self.outgoing[array].at[slot],
            self.far[array].at[slot],
            self.far_sems[0].at[array, slot],
            self.far_sems[1].at[array, slot],
            {"dp": device},
        )

    def kv_copy(self, slot):
        return send(
            self.staged.at[self.others[slot]],
            self.arrived.at[slot],
            self.kv_sems[0].at[slot],
            self.kv_sems[1].at[slot],
            {"tensor": self.others[slot]},
        )

    def tile_copy(self, slot):
        return send(
            self.gain_tile,
            self.gain_near.at[slot],
            self.tile_sems[0].at[slot],
            self.tile_sems[1].at[slot],
            {"tensor": self.others[slot]},
        )

    def mid_copy(self, slot):
        return send(
            self.gain_mid,
            self.gain_far.at[slot],
            self.mid_sems[0].at[slot],
            self.mid_sems[1].at[slot],
            {"dp": self.peers[slot]},
        )

    def pair_sum(self, array, block):
        self.near_copy(array, block).wait_recv()
        own = self.grads[array][2 * block + self.parity].astype(jnp.float32)
        return own + self.got[array][block].astype(jnp.float32)

    def advance(self, step):
        shifts = [self.half // 2] + [shift for shift in range(1, self.half) if shift != self.half // 2]
        if step == 0:
            for shift in shifts + [0]:
                for array in (0, 1):
                    self.begin(self.near_copy(array, (self.row + shift) % self.half))
        elif step in (1, 2, 3):
            for shift in shifts[step - 1 :: 3]:
                for array in (0, 1):
                    total = self.pair_sum(array, (self.row + shift) % self.half)
                    self.outgoing[array][shift - 1] = total.astype(jnp.bfloat16)
                    self.begin(self.far_copy(array, shift))
        elif step == 6:
            self.gain_tile[...] = self.gain_rows[...]
            self.gain_tile[0:1, :] = self.sums[0][...]
            for slot in range(3):
                self.begin(self.tile_copy(slot))
        elif step == 7:
            for array in (0, 1):
                total = self.pair_sum(array, self.row)
                for shift in shifts:
                    self.far_copy(array, shift).wait_recv()
                    total = total + self.far[array][shift - 1].astype(jnp.float32)
                if array == 0:
                    self.mixed_sum[...] = total
                    first, each = self.query_part.shape[1], self.kv_part.shape[1]
                    self.query_part[...] = self.mixed_sum[:, pl.ds(0, first)]
                    for device in range(4):
                        self.staged[device] = self.mixed_sum[:, pl.ds(first + each * device, each)]
                    for slot in range(3):
                        self.begin(self.kv_copy(slot))
                else:
                    self.output_part[...] = total
        elif step == 8:
            total = self.gain_tile[...]
            for slot in range(3):
                self.tile_copy(slot).wait_recv()
                total = total + self.gain_near[slot]
            self.gain_mid[...] = total
            for slot in range(self.count - 1):
                self.begin(self.mid_copy(slot))
        elif step == 9:
            total = self.staged[self.me]
            for slot in range(3):
                self.kv_copy(slot).wait_recv()
                total = total + self.arrived[slot]
            self.kv_part[...] = total
            total = self.gain_mid[...]
            for slot in range(self.count - 1):
                self.mid_copy(slot).wait_recv()
                total = total + self.gain_far[slot]
            self.gain_sum[...] = total

    def finish(self):
        for copy in self.sent:
            copy.wait_send()


class FinalRider:
    pace = 1

    def __init__(self, mixed, output, gain_rows, query_columns, count):
        rows, half = mixed.shape[1], count // 2
        each = (mixed.shape[2] - query_columns) // 4
        columns = (mixed.shape[2], output.shape[2])
        self.arrays, self.inputs, self.outputs = (mixed, output, gain_rows), 3, 4
        self.shapes = [
            jax.ShapeDtypeStruct((rows, query_columns), jnp.float32),
            jax.ShapeDtypeStruct((rows, each), jnp.float32),
            jax.ShapeDtypeStruct((rows, columns[1]), jnp.float32),
            jax.ShapeDtypeStruct(gain_rows.shape, jnp.float32),
        ]
        self.scratch = [pltpu.VMEM((half, rows, size), jnp.bfloat16) for size in columns]
        self.scratch += [pltpu.VMEM((half - 1, rows, size), jnp.bfloat16) for size in columns * 2]
        self.scratch += [
            pltpu.VMEM((rows, columns[0]), jnp.float32),
            pltpu.VMEM((4, rows, each), jnp.float32),
            pltpu.VMEM((3, rows, each), jnp.float32),
            pltpu.VMEM(gain_rows.shape, jnp.float32),
            pltpu.VMEM((3,) + gain_rows.shape, jnp.float32),
            pltpu.VMEM(gain_rows.shape, jnp.float32),
            pltpu.VMEM((count - 1,) + gain_rows.shape, jnp.float32),
        ]
        for shape in ((2, half), (2, half - 1), (3,), (3,), (count - 1,)):
            self.scratch += [pltpu.SemaphoreType.DMA(shape)] * 2

    def build(self, inputs, outputs, scratch, count):
        return FinalExchange(inputs, outputs, scratch, count)

    def prepare(self, inputs, outputs):
        pass


def joint_kernel(row_map, extra_count, row_count, sum_count, spreads, rider, count, *refs):
    refs = list(refs)

    def take(number):
        taken = refs[:number]
        del refs[:number]
        return taken

    (partial,) = take(1)
    extras = take(extra_count)
    (gains,) = take(1)
    rider_in = take(rider.inputs)
    gathered = take(1)[0] if spreads else None
    row_outs = take(row_count)
    sum_outs = take(sum_count)
    rider_out = take(rider.outputs)
    near, outgoing, far, send_sems, recv_sems = take(5)
    if spreads:
        spread_send, spread_recv = take(2)
    ring = rider.build(rider_in, rider_out, refs, count)
    ring.sums = sum_outs
    me, mate, across, diagonal = tensor_peers()
    rows_each = partial.shape[1] // chunk_count
    greet([{"tensor": mate}, {"tensor": across}] + ring.targets())
    ring_steps = list(ring.steps())

    def ride():
        if ring_steps:
            ring.advance(ring_steps.pop(0))


    def near_copy(flow, chunk):
        owner = mate if flow else diagonal
        part = pl.ds(chunk * rows_each, rows_each)
        return send(
            partial.at[owner, part], near.at[flow, part], send_sems.at[flow, chunk], recv_sems.at[flow, chunk], {"tensor": mate}
        )

    def far_copy(chunk):
        part = pl.ds(chunk * rows_each, rows_each)
        return send(outgoing.at[part], far.at[part], send_sems.at[2, chunk], recv_sems.at[2, chunk], {"tensor": across})

    for flow in (0, 1):
        for chunk in range(chunk_count):
            near_copy(flow, chunk).start()
    rider.prepare(rider_in, rider_out)
    ride()
    for chunk in range(chunk_count):
        part = pl.ds(chunk * rows_each, rows_each)
        near_copy(0, chunk).wait_recv()
        total = partial[across, part, :].astype(jnp.float32) + near[0, part, :].astype(jnp.float32)
        outgoing[part, :] = total.astype(jnp.bfloat16)
        far_copy(chunk).start()
    ride()
    if spreads:
        spread = Spread(gathered, spread_send, spread_recv, rows_each)
    sums = None
    for chunk in range(chunk_count):
        part = pl.ds(chunk * rows_each, rows_each)
        near_copy(1, chunk).wait_recv()
        total = partial[me, part, :].astype(jnp.float32) + near[1, part, :].astype(jnp.float32)
        far_copy(chunk).wait_recv()
        total = total + far[part, :].astype(jnp.float32)
        given, rows_out, sums_out = row_map(total, [extra[part, :] for extra in extras], gains)
        if spreads:
            gathered[me, part, :] = given.astype(jnp.bfloat16)
            spread.give(chunk)
        for ref, value in zip(row_outs, rows_out):
            ref[part, :] = value.astype(ref.dtype)
        sums = sums_out if sums is None else [held + new for held, new in zip(sums, sums_out)]
        if spreads and chunk > 0:
            spread.forward(chunk - 1)
        if chunk % rider.pace == rider.pace - 1:
            ride()
    for ref, value in zip(sum_outs, sums):
        ref[...] = value
    if spreads:
        spread.forward(chunk_count - 1)
    while ring_steps:
        ride()
    if spreads:
        spread.finish(chunk_count)
    for chunk in range(chunk_count):
        near_copy(0, chunk).wait_send()
        near_copy(1, chunk).wait_send()
        far_copy(chunk).wait_send()
    ring.finish()


def joint(row_map, partial, extras, gains, row_types, sum_count, spreads, rider, count, collective_id):
    rows, width = partial.shape[0] // 4, partial.shape[1]
    outputs = []
    if spreads:
        outputs.append(jax.ShapeDtypeStruct((4, rows, width), jnp.bfloat16))
    outputs += [jax.ShapeDtypeStruct((rows, width), kind) for kind in row_types]
    outputs += [jax.ShapeDtypeStruct((1, width), jnp.float32)] * sum_count
    outputs += rider.shapes
    scratch = [
        pltpu.VMEM((2, rows, width), jnp.bfloat16),
        pltpu.VMEM((rows, width), jnp.bfloat16),
        pltpu.VMEM((rows, width), jnp.bfloat16),
        pltpu.SemaphoreType.DMA((3, chunk_count)),
        pltpu.SemaphoreType.DMA((3, chunk_count)),
    ]
    if spreads:
        scratch += [pltpu.SemaphoreType.DMA((3, chunk_count))] * 2
    scratch += rider.scratch
    found = list(call(
        functools.partial(joint_kernel, row_map, len(extras), len(row_types), sum_count, spreads, rider, count),
        (partial.reshape(4, rows, width),) + tuple(extras) + (gains,) + tuple(rider.arrays),
        outputs,
        scratch,
        collective_id,
    ))
    if spreads:
        found[0] = found[0].reshape(4 * rows, width)
    return found


def branch_map(branch, extras, gains):
    middle = extras[0].astype(jnp.float32) + norm_rows(branch, gains[1:2, :])
    return norm_rows(middle, gains[2:3, :]), [branch, middle], []


def ffn_map(ffn_out, extras, gains):
    middle, cotangent = extras
    outcome = middle + norm_rows(ffn_out, gains[3:4, :])
    grad_ffn, gain_last = norm_pull(ffn_out, gains[3:4, :], cotangent.astype(jnp.float32))
    return grad_ffn, [outcome], [gain_last]


def middle_map(grad_mid_normed, extras, gains):
    middle, branch, cotangent = extras
    pulled, gain_mid = norm_pull(middle, gains[2:3, :], grad_mid_normed)
    grad_middle = cotangent.astype(jnp.float32) + pulled
    grad_branch, gain_branch = norm_pull(branch, gains[1:2, :], grad_middle)
    return grad_branch, [grad_middle], [gain_branch, gain_mid]


def first_map(grad_first_normed, extras, gains):
    tokens, grad_middle = extras
    pulled, gain_first = norm_pull(tokens.astype(jnp.float32), gains[0:1, :], grad_first_normed)
    return None, [grad_middle + pulled], [gain_first]


def hand_over_kernel(*refs):
    number = len(refs) // 2
    for source, target in zip(refs[:number], refs[number:]):
        target[...] = source[...]


def hand_over(*arrays):
    return pl.pallas_call(
        hand_over_kernel, out_shape=[jax.ShapeDtypeStruct(array.shape, array.dtype) for array in arrays]
    )(*arrays)


def body(
    tokens,
    segments,
    query_weight,
    keyvalue_weight,
    output_weight,
    gate_weight,
    up_weight,
    down_weight,
    norm_gains,
    headnorm_gains,
    cotangent,
):
    head_width = headnorm_gains.shape[1]
    width = tokens.shape[1]
    hidden_width = gate_weight.shape[1]
    count = lax.axis_size("dp")
    own_rows = query_weight.shape[0]
    padded_rows = -(-own_rows // 16) * 16
    seg_tile = segments.reshape(-1, 128)
    rows_all, segment_all, full = opening(
        tokens, seg_tile, norm_gains, (query_weight, keyvalue_weight, output_weight.T), padded_rows, count
    )
    rows_all = rows_all.reshape(-1, width)
    segment_all = segment_all.reshape(-1)

    def join_blocks(blocks):
        return blocks[:, :own_rows].reshape(width, -1)

    def cut_blocks(whole):
        blocks = whole.astype(jnp.bfloat16).reshape(count, own_rows, -1)
        return jnp.pad(blocks, ((0, 0), (0, padded_rows - own_rows), (0, 0)))

    full = join_blocks(full)
    mixed_full = full[:, : 3 * head_width]
    output_full = full[:, 3 * head_width :]
    length = rows_all.shape[0]
    block_rows = min(512, length)
    cosine_table, sine_table = angles(length, head_width)

    def query_map(raw_values, scaling):
        return rotate(norm_rows(raw_values, scaling), cosine_table, sine_table) * score_scale

    def key_map(raw_values, scaling):
        return rotate(norm_rows(raw_values, scaling), cosine_table, sine_table)

    mixed_raw = dot_rows(rows_all, mixed_full)
    query_raw = mixed_raw[:, :head_width]
    keyvalue_raw = mixed_raw[:, head_width:]
    query_rows = query_map(query_raw, headnorm_gains[0]).astype(jnp.bfloat16)
    key_rows = key_map(keyvalue_raw[:, :head_width], headnorm_gains[1]).astype(jnp.bfloat16)
    value_rows = keyvalue_raw[:, head_width:].astype(jnp.bfloat16)

    def masked_scores(row_from, row_to):
        scores = dot_inner(query_rows[row_from:row_to], key_rows[:row_to])
        row_places = row_from + jnp.arange(row_to - row_from)
        key_places = jnp.arange(row_to)
        allowed = (key_places[None, :] <= row_places[:, None]) & (
            segment_all[row_from:row_to][:, None] == segment_all[:row_to][None, :]
        )
        return jnp.where(allowed, scores, -jnp.inf)

    pieces_out = []
    pieces_total = []
    for block_id in range(length // block_rows):
        row_from = block_id * block_rows
        row_to = row_from + block_rows
        scores = masked_scores(row_from, row_to)
        row_peak = jnp.max(scores, axis=-1, keepdims=True)
        raised = jnp.exp(scores - row_peak)
        row_total = jnp.sum(raised, axis=-1, keepdims=True)
        weights_low = (raised / row_total).astype(jnp.bfloat16)
        pieces_out.append(dot_rows(weights_low, value_rows[:row_to]).astype(jnp.bfloat16))
        pieces_total.append(row_peak + jnp.log(row_total))
    attended = jnp.concatenate(pieces_out, axis=0)
    log_totals = jnp.concatenate(pieces_total, axis=0)
    branch_partial = dot_inner(attended, output_full).astype(jnp.bfloat16)
    carried = GatherRider((gate_weight, up_weight, down_weight.T), padded_rows, count)
    mid_all, branch, middle, full = joint(
        branch_map, branch_partial, (tokens,), norm_gains, (jnp.float32, jnp.float32), 0, True, carried, count, 1
    )
    full = join_blocks(full)
    pair_full = full[:, : 2 * hidden_width]
    down_full = full[:, 2 * hidden_width :]
    paired = dot_rows(mid_all, pair_full)
    gating = paired[:, :hidden_width]
    upward = paired[:, hidden_width:]
    idle = IdleRider(count)
    hidden = activate(gating, upward).astype(jnp.bfloat16)
    ffn_partial = dot_inner(hidden, down_full).astype(jnp.bfloat16)
    grad_ffn_all, outcome, gain_last = joint(
        ffn_map, ffn_partial, (middle, cotangent), norm_gains, (jnp.bfloat16,), 1, True, idle, count, 2
    )
    grad_hidden = dot_rows(grad_ffn_all, down_full)
    down_grad = cut_blocks(dot_outer(grad_ffn_all, hidden))
    ignored, pull_active = jax.vjp(activate, gating, upward)
    grad_gating, grad_upward = pull_active(grad_hidden)
    paired_low = jnp.concatenate(
        [grad_gating.astype(jnp.bfloat16), grad_upward.astype(jnp.bfloat16)], axis=1
    )
    mid_partial = dot_inner(paired_low, pair_full).astype(jnp.bfloat16)
    pair_grad = cut_blocks(dot_outer(mid_all, paired_low))
    down_half = hidden_width // 2
    plan = (
        (0, 0, 0, hidden_width, 0, 0),
        (1, 0, hidden_width, hidden_width, 1, 0),
        (0, 1, 0, down_half, 2, 0),
        (1, 1, down_half, down_half, 2, down_half),
    )
    carried = ReduceRider((pair_grad, down_grad), plan, (hidden_width,) * 3, count)
    branch_all, grad_middle, gain_branch, gain_mid, gate_part, up_part, down_part = joint(
        middle_map, mid_partial, (middle, branch, cotangent), norm_gains, (jnp.float32,), 2, True, carried, count, 3
    )
    output_grad = cut_blocks(dot_outer(branch_all, attended))
    grad_attended = dot_rows(branch_all, output_full).astype(jnp.bfloat16)
    grad_query_parts = []
    grad_keys = jnp.zeros((length, head_width), jnp.float32)
    grad_values = jnp.zeros((length, head_width), jnp.float32)
    for block_id in range(length // block_rows):
        row_from = block_id * block_rows
        row_to = row_from + block_rows
        scores = masked_scores(row_from, row_to)
        weights_full = jnp.exp(scores - log_totals[row_from:row_to])
        weights_low = weights_full.astype(jnp.bfloat16)
        grad_block = grad_attended[row_from:row_to]
        grad_weights = dot_inner(grad_block, value_rows[:row_to])
        row_inner = jnp.sum(weights_full * grad_weights, axis=-1, keepdims=True)
        grad_scores = (weights_full * (grad_weights - row_inner)).astype(jnp.bfloat16)
        grad_query_parts.append(dot_rows(grad_scores, key_rows[:row_to]))
        grad_keys = grad_keys.at[:row_to].add(dot_outer(grad_scores, query_rows[row_from:row_to]))
        grad_values = grad_values.at[:row_to].add(dot_outer(weights_low, grad_block))
    grad_query = jnp.concatenate(grad_query_parts, axis=0)
    ignored, pull_query = jax.vjp(query_map, query_raw, headnorm_gains[0])
    grad_query_raw, gain_query = pull_query(grad_query)
    ignored, pull_key = jax.vjp(key_map, keyvalue_raw[:, :head_width], headnorm_gains[1])
    grad_key_raw, gain_key = pull_key(grad_keys)
    mixed_low = jnp.concatenate([grad_query_raw, grad_key_raw, grad_values], axis=1).astype(jnp.bfloat16)
    first_partial = dot_inner(mixed_low, mixed_full).astype(jnp.bfloat16)
    mixed_grad = cut_blocks(dot_outer(rows_all, mixed_low))
    head_rows = jnp.pad(jnp.stack([gain_query, gain_key]), ((0, 2), (0, width - head_width)))
    gain_rows = jnp.concatenate([jnp.zeros_like(gain_last), gain_branch, gain_mid, gain_last, head_rows], axis=0)
    carried = FinalRider(mixed_grad, output_grad, gain_rows, head_width, count)
    grad_tokens, gain_first, query_part, keyvalue_part, output_part, gain_sum = joint(
        first_map, first_partial, (tokens, grad_middle), norm_gains, (jnp.float32,), 1, False, carried, count, 4
    )
    me = lax.axis_index("tensor")
    mine = lax.axis_index("dp")
    gains_part = lax.dynamic_slice(gain_sum, (me, mine * own_rows), (1, own_rows))
    head_own = head_width // (count * 4)
    heads_part = lax.dynamic_slice(gain_sum, (4, (mine * 4 + me) * head_own), (2, head_own))
    outcome, grad_tokens, query_part, keyvalue_part, gate_part, up_part = hand_over(
        outcome,
        grad_tokens,
        query_part[:own_rows],
        keyvalue_part[:own_rows],
        gate_part[:own_rows],
        up_part[:own_rows],
    )
    return (
        outcome,
        grad_tokens,
        query_part,
        keyvalue_part,
        output_part[:own_rows].T,
        gate_part,
        up_part,
        down_part[:own_rows].T,
        gains_part,
        heads_part,
    )


def solution(mesh):
    placed = (
        P(("dp", "tensor"), None),
        P(("dp", "tensor")),
        P("dp", "tensor"),
        P("dp", None),
        P("tensor", "dp"),
        P("dp", "tensor"),
        P("dp", "tensor"),
        P("tensor", "dp"),
        P(),
        P(),
        P(("dp", "tensor"), None),
    )
    return jax.shard_map(
        body,
        mesh=mesh,
        in_specs=placed,
        out_specs=(
            P(("dp", "tensor"), None),
            P(("dp", "tensor"), None),
            P("dp", "tensor"),
            P("dp", "tensor"),
            P("tensor", "dp"),
            P("dp", "tensor"),
            P("dp", "tensor"),
            P("tensor", "dp"),
            P("tensor", "dp"),
            P(None, ("dp", "tensor")),
        ),
        check_vma=False,
    )
```

```python
import functools

import jax
import jax.numpy as jnp
from jax import lax
from jax.experimental import pallas as pl
from jax.experimental.pallas import tpu as pltpu
from jax.sharding import PartitionSpec as P

epsilon = 1e-06
rope_base = 1000000.0
score_scale = 0.0625
MESH = pl.DeviceIdType.MESH
chunk_count = 4
vmem_bytes = 56 * 2**20
in_vmem = pl.BlockSpec(memory_space=pltpu.VMEM)


def norm_rows(values, scaling):
    return values * lax.rsqrt(jnp.mean(values * values, axis=-1, keepdims=True) + epsilon) * scaling


def norm_pull(values, scaling, grad):
    inverse = lax.rsqrt(jnp.mean(values * values, axis=-1, keepdims=True) + epsilon)
    scaled = grad * scaling
    inner = jnp.mean(values * scaled, axis=-1, keepdims=True)
    pulled = inverse * scaled - values * (inverse * inverse * inverse * inner)
    return pulled, jnp.sum(grad * values * inverse, axis=0, keepdims=True)


def angles(length, head_width):
    halfway = head_width // 2
    places = jnp.arange(length, dtype=jnp.float32)[:, None]
    frequency = rope_base ** (-2.0 * jnp.arange(halfway, dtype=jnp.float32) / head_width)
    phases = places * frequency[None, :]
    return (jnp.cos(phases), jnp.sin(phases))


def rotate(values, cosine_table, sine_table):
    halfway = values.shape[-1] // 2
    leading = values[..., :halfway]
    trailing = values[..., halfway:]
    return jnp.concatenate(
        [
            leading * cosine_table - trailing * sine_table,
            trailing * cosine_table + leading * sine_table,
        ],
        axis=-1,
    )


def activate(gating, upward):
    return jax.nn.gelu(gating, approximate=True) * upward


def dot_rows(left_side, right_side):
    return jnp.dot(left_side, right_side, preferred_element_type=jnp.float32)


def dot_inner(left_side, right_side):
    return lax.dot_general(
        left_side, right_side, (((1,), (1,)), ((), ())), preferred_element_type=jnp.float32
    )


def dot_outer(left_side, right_side):
    return lax.dot_general(
        left_side, right_side, (((0,), (0,)), ((), ())), preferred_element_type=jnp.float32
    )


def send(source, target, send_sem, recv_sem, device):
    return pltpu.make_async_remote_copy(
        src_ref=source,
        dst_ref=target,
        send_sem=send_sem,
        recv_sem=recv_sem,
        device_id=device,
        device_id_type=MESH,
    )


def tensor_peers():
    me = lax.axis_index("tensor")
    chip = me // 2
    core = me % 2
    mate = chip * 2 + 1 - core
    across = (1 - chip) * 2 + core
    diagonal = (1 - chip) * 2 + 1 - core
    return me, mate, across, diagonal


def ring_place(index, count):
    odd = index % 2
    return (index // 2) * (1 - odd) + (count - 1 - index // 2) * odd


def ring_index(place, count):
    back = place // (count // 2)
    return (2 * place) * (1 - back) + (2 * (count - 1 - place) + 1) * back


def greet(targets):
    barrier = pltpu.get_barrier_semaphore()
    for target in targets:
        pl.semaphore_signal(barrier, inc=1, device_id=target, device_id_type=MESH)
    pl.semaphore_wait(barrier, len(targets))


def call(kernel, arguments, outputs, scratch, collective_id):
    return pl.pallas_call(
        kernel,
        out_shape=outputs,
        in_specs=[in_vmem] * len(arguments),
        out_specs=[in_vmem] * len(outputs),
        scratch_shapes=scratch,
        compiler_params=pltpu.CompilerParams(
            collective_id=collective_id, has_side_effects=True, vmem_limit_bytes=vmem_bytes
        ),
    )(*arguments)


class Spread:
    def __init__(self, gathered, send_sems, recv_sems, rows):
        self.gathered, self.send_sems, self.recv_sems, self.rows = gathered, send_sems, recv_sems, rows
        self.me, self.mate, self.across, self.diagonal = tensor_peers()
        self.sent = []

    def copy(self, flow, owner, chunk, device):
        part = self.gathered.at[owner, pl.ds(chunk * self.rows, self.rows)]
        return send(
            part, part, self.send_sems.at[flow, chunk], self.recv_sems.at[flow, chunk], {"tensor": device}
        )

    def give(self, chunk):
        for flow, device in ((0, self.across), (1, self.mate)):
            copy = self.copy(flow, self.me, chunk, device)
            copy.start()
            self.sent.append(copy)

    def forward(self, chunk):
        self.copy(0, self.across, chunk, self.across).wait_recv()
        copy = self.copy(2, self.across, chunk, self.mate)
        copy.start()
        self.sent.append(copy)

    def finish(self, chunks):
        for chunk in range(chunks):
            self.copy(1, self.mate, chunk, self.mate).wait_recv()
            self.copy(2, self.diagonal, chunk, self.mate).wait_recv()
        for copy in self.sent:
            copy.wait_send()


def ring_peers(count):
    place = ring_place(lax.axis_index("dp"), count)
    right = ring_index((place + 1) % count, count)
    left = ring_index((place + count - 1) % count, count)
    return place, right, left


class RingGather:
    def __init__(self, full, send_sems, recv_sems, count):
        self.full, self.send_sems, self.recv_sems, self.count = full, send_sems, recv_sems, count
        self.place, self.right, self.left = ring_peers(count)
        self.last = count // 2 - 1
        self.sent = []

    def copy(self, way, step, owner):
        part = self.full.at[owner]
        if step == self.last:
            half = self.full.shape[2] // 2
            part = self.full.at[owner, :, pl.ds(half * way, half)]
        device = {"dp": self.left if way else self.right}
        return send(part, part, self.send_sems.at[way, step], self.recv_sems.at[way, step], device)

    def owner(self, way, step):
        shift = step if way else self.count - step
        return ring_index((self.place + shift) % self.count, self.count)

    def targets(self):
        return [{"dp": self.right}, {"dp": self.left}]

    def steps(self):
        return range(self.last + 2)

    def advance(self, step):
        for way in (0, 1):
            if step > 0:
                self.copy(way, step - 1, self.owner(way, step)).wait_recv()
            if step <= self.last:
                copy = self.copy(way, step, self.owner(way, step))
                copy.start()
                self.sent.append(copy)

    def finish(self):
        for copy in self.sent:
            copy.wait_send()


class RingReduce:
    def __init__(self, flows, slots, send_sems, recv_sems, count):
        self.flows, self.slots, self.send_sems, self.recv_sems, self.count = flows, slots, send_sems, recv_sems, count
        self.place, self.right, self.left = ring_peers(count)

    def chunk(self, way, step):
        shift = 1 + step if way else 2 * self.count - 1 - step
        return ring_index((self.place + shift) % self.count, self.count)

    def copy(self, flow, step):
        way, grads, start, size = self.flows[flow][:4]
        if step == 0:
            source = grads.at[self.chunk(way, 0), :, pl.ds(start, size)]
        else:
            source = self.slots[flow].at[step - 1]
        device = {"dp": self.left if way else self.right}
        return send(
            source, self.slots[flow].at[step], self.send_sems.at[flow, step], self.recv_sems.at[flow, step], device
        )

    def targets(self):
        return [{"dp": self.right}, {"dp": self.left}]

    def steps(self):
        return range(self.count)

    def advance(self, step):
        for flow, (way, grads, start, size, target, place) in enumerate(self.flows):
            if step == 0:
                self.copy(flow, 0).start()
                continue
            self.copy(flow, step - 1).wait_recv()
            own = grads[self.chunk(way, step), :, pl.ds(start, size)].astype(jnp.float32)
            total = self.slots[flow][step - 1].astype(jnp.float32) + own
            if step < self.count - 1:
                self.slots[flow][step - 1] = total.astype(jnp.bfloat16)
                self.copy(flow, step).start()
            else:
                target[:, pl.ds(place, size)] = total

    def finish(self):
        for step in range(self.count - 1):
            for flow in range(len(self.flows)):
                self.copy(flow, step).wait_send()


def reduce_scratch(flow_sizes, rows, count):
    slots = [pltpu.VMEM((count - 1, rows, size), jnp.bfloat16) for size in flow_sizes]
    return slots + [pltpu.SemaphoreType.DMA((len(flow_sizes), count - 1))] * 2


def gather_scratch(count):
    return [pltpu.SemaphoreType.DMA((2, count // 2))] * 2


def place_shard(full, weights, mine):
    start = 0
    for weight in weights:
        full[mine, pl.ds(0, weight.shape[0]), pl.ds(start, weight.shape[1])] = weight[...]
        start += weight.shape[1]


def gathered_shape(weights, padded_rows, count):
    columns = sum(weight.shape[1] for weight in weights)
    return jax.ShapeDtypeStruct((count, padded_rows, columns), jnp.bfloat16)


def opening_kernel(
    count, tokens, segments, gains, first, second, third, rows_all, segment_all, full, send_sems, recv_sems, seg_send, seg_recv, ring_send, ring_recv
):
    me, mate, across, diagonal = tensor_peers()
    ring = RingGather(full, ring_send, ring_recv, count)
    greet([{"tensor": mate}, {"tensor": across}, {"tensor": diagonal}, {"dp": ring.right}, {"dp": ring.left}])
    place_shard(full, (first, second, third), lax.axis_index("dp"))
    ring.advance(0)
    segment_all[me] = segments[...]
    spread = Spread(rows_all, send_sems, recv_sems, tokens.shape[0] // chunk_count)
    for chunk in range(chunk_count):
        rows = pl.ds(chunk * spread.rows, spread.rows)
        normed = norm_rows(tokens[rows, :].astype(jnp.float32), gains[0:1, :])
        rows_all[me, rows, :] = normed.astype(jnp.bfloat16)
        spread.give(chunk)
    seg_sent = []
    for flow, device in enumerate((mate, across, diagonal)):
        part = segment_all.at[me]
        copy = send(part, part, seg_send.at[flow], seg_recv.at[flow], {"tensor": device})
        copy.start()
        seg_sent.append(copy)
    ring.advance(1)
    for chunk in range(chunk_count):
        spread.forward(chunk)
    for step in ring.steps()[2:]:
        ring.advance(step)
    spread.finish(chunk_count)
    for flow, device in enumerate((mate, across, diagonal)):
        part = segment_all.at[device]
        send(part, part, seg_send.at[flow], seg_recv.at[flow], {"tensor": device}).wait_recv()
    for copy in seg_sent:
        copy.wait_send()
    ring.finish()


def opening(tokens, segments, gains, weights, padded_rows, count):
    rows, width = tokens.shape
    return call(
        functools.partial(opening_kernel, count),
        (tokens, segments, gains) + weights,
        [
            jax.ShapeDtypeStruct((4, rows, width), jnp.bfloat16),
            jax.ShapeDtypeStruct((4,) + segments.shape, jnp.int32),
            gathered_shape(weights, padded_rows, count),
        ],
        [
            pltpu.SemaphoreType.DMA((3, chunk_count)),
            pltpu.SemaphoreType.DMA((3, chunk_count)),
            pltpu.SemaphoreType.DMA((3,)),
            pltpu.SemaphoreType.DMA((3,)),
        ]
        + gather_scratch(count),
        0,
    )


class IdleRider:
    pace, arrays, inputs, outputs, shapes, scratch = 1, (), 0, 0, [], []

    def __init__(self, count):
        self.count = count

    def build(self, inputs, outputs, scratch, count):
        return self

    def steps(self):
        return ()

    def targets(self):
        return []

    def prepare(self, inputs, outputs):
        pass

    def finish(self):
        pass


class GatherRider:
    pace = 2

    def __init__(self, weights, padded_rows, count):
        self.arrays, self.inputs, self.outputs = weights, len(weights), 1
        self.shapes = [gathered_shape(weights, padded_rows, count)]
        self.scratch = gather_scratch(count)

    def build(self, inputs, outputs, scratch, count):
        return RingGather(outputs[0], scratch[0], scratch[1], count)

    def prepare(self, inputs, outputs):
        place_shard(outputs[0], inputs, lax.axis_index("dp"))


class ReduceRider:
    pace = 1

    def __init__(self, grads, plan, out_columns, count):
        rows = grads[0].shape[1]
        self.arrays, self.inputs, self.outputs, self.plan = grads, len(grads), len(out_columns), plan
        self.shapes = [jax.ShapeDtypeStruct((rows, columns), jnp.float32) for columns in out_columns]
        self.scratch = reduce_scratch([flow[3] for flow in plan], rows, count)

    def build(self, inputs, outputs, scratch, count):
        flows = [(way, inputs[a], start, size, outputs[o], at) for way, a, start, size, o, at in self.plan]
        number = len(flows)
        return RingReduce(flows, scratch[:number], scratch[number], scratch[number + 1], count)

    def prepare(self, inputs, outputs):
        pass


class FinalExchange:
    def __init__(self, inputs, outputs, scratch, count):
        self.grads, self.gain_rows = inputs[:2], inputs[2]
        self.query_part, self.kv_part, self.output_part, self.gain_sum = outputs
        self.got, self.outgoing, self.far = scratch[0:2], scratch[2:4], scratch[4:6]
        self.mixed_sum, self.staged, self.arrived = scratch[6:9]
        self.gain_tile, self.gain_near, self.gain_mid, self.gain_far = scratch[9:13]
        self.near_sems, self.far_sems, self.kv_sems, self.tile_sems, self.mid_sems = [
            scratch[at : at + 2] for at in range(13, 23, 2)
        ]
        self.count, self.half = count, count // 2
        self.mine = lax.axis_index("dp")
        self.row, self.parity = self.mine // 2, self.mine % 2
        self.partner = self.row * 2 + 1 - self.parity
        self.me = lax.axis_index("tensor")
        self.others = [(self.me + shift) % 4 for shift in (1, 2, 3)]
        self.peers = [(self.mine + shift) % count for shift in range(1, count)]
        self.sent = []

    def targets(self):
        return [{"dp": peer} for peer in self.peers] + [{"tensor": tensor_peers()[3]}]

    def steps(self):
        return range(10)

    def begin(self, copy):
        copy.start()
        self.sent.append(copy)

    def near_copy(self, array, block):
        return send(
            self.grads[array].at[2 * block + 1 - self.parity],
            self.got[array].at[block],
            self.near_sems[0].at[array, block],
            self.near_sems[1].at[array, block],
            {"dp": self.partner},
        )

    def far_copy(self, array, shift):
        device = 2 * ((self.row + shift) % self.half) + self.parity
        slot = shift - 1
        return send(
            self.outgoing[array].at[slot],
            self.far[array].at[slot],
            self.far_sems[0].at[array, slot],
            self.far_sems[1].at[array, slot],
            {"dp": device},
        )

    def kv_copy(self, slot):
        return send(
            self.staged.at[self.others[slot]],
            self.arrived.at[slot],
            self.kv_sems[0].at[slot],
            self.kv_sems[1].at[slot],
            {"tensor": self.others[slot]},
        )

    def tile_copy(self, slot):
        return send(
            self.gain_tile,
            self.gain_near.at[slot],
            self.tile_sems[0].at[slot],
            self.tile_sems[1].at[slot],
            {"tensor": self.others[slot]},
        )

    def mid_copy(self, slot):
        return send(
            self.gain_mid,
            self.gain_far.at[slot],
            self.mid_sems[0].at[slot],
            self.mid_sems[1].at[slot],
            {"dp": self.peers[slot]},
        )

    def pair_sum(self, array, block):
        self.near_copy(array, block).wait_recv()
        own = self.grads[array][2 * block + self.parity].astype(jnp.float32)
        return own + self.got[array][block].astype(jnp.float32)

    def advance(self, step):
        shifts = [self.half // 2] + [shift for shift in range(1, self.half) if shift != self.half // 2]
        if step == 0:
            for shift in shifts + [0]:
                for array in (0, 1):
                    self.begin(self.near_copy(array, (self.row + shift) % self.half))
        elif step in (1, 2, 3):
            for shift in shifts[step - 1 :: 3]:
                for array in (0, 1):
                    total = self.pair_sum(array, (self.row + shift) % self.half)
                    self.outgoing[array][shift - 1] = total.astype(jnp.bfloat16)
                    self.begin(self.far_copy(array, shift))
        elif step == 6:
            self.gain_tile[...] = self.gain_rows[...]
            self.gain_tile[0:1, :] = self.sums[0][...]
            for slot in range(3):
                self.begin(self.tile_copy(slot))
        elif step == 7:
            for array in (0, 1):
                total = self.pair_sum(array, self.row)
                for shift in shifts:
                    self.far_copy(array, shift).wait_recv()
                    total = total + self.far[array][shift - 1].astype(jnp.float32)
                if array == 0:
                    self.mixed_sum[...] = total
                    first, each = self.query_part.shape[1], self.kv_part.shape[1]
                    self.query_part[...] = self.mixed_sum[:, pl.ds(0, first)]
                    for device in range(4):
                        self.staged[device] = self.mixed_sum[:, pl.ds(first + each * device, each)]
                    for slot in range(3):
                        self.begin(self.kv_copy(slot))
                else:
                    self.output_part[...] = total
        elif step == 8:
            total = self.gain_tile[...]
            for slot in range(3):
                self.tile_copy(slot).wait_recv()
                total = total + self.gain_near[slot]
            self.gain_mid[...] = total
            for slot in range(self.count - 1):
                self.begin(self.mid_copy(slot))
        elif step == 9:
            total = self.staged[self.me]
            for slot in range(3):
                self.kv_copy(slot).wait_recv()
                total = total + self.arrived[slot]
            self.kv_part[...] = total
            total = self.gain_mid[...]
            for slot in range(self.count - 1):
                self.mid_copy(slot).wait_recv()
                total = total + self.gain_far[slot]
            self.gain_sum[...] = total

    def finish(self):
        for copy in self.sent:
            copy.wait_send()


class FinalRider:
    pace = 1

    def __init__(self, mixed, output, gain_rows, query_columns, count):
        rows, half = mixed.shape[1], count // 2
        each = (mixed.shape[2] - query_columns) // 4
        columns = (mixed.shape[2], output.shape[2])
        self.arrays, self.inputs, self.outputs = (mixed, output, gain_rows), 3, 4
        self.shapes = [
            jax.ShapeDtypeStruct((rows, query_columns), jnp.float32),
            jax.ShapeDtypeStruct((rows, each), jnp.float32),
            jax.ShapeDtypeStruct((rows, columns[1]), jnp.float32),
            jax.ShapeDtypeStruct(gain_rows.shape, jnp.float32),
        ]
        self.scratch = [pltpu.VMEM((half, rows, size), jnp.bfloat16) for size in columns]
        self.scratch += [pltpu.VMEM((half - 1, rows, size), jnp.bfloat16) for size in columns * 2]
        self.scratch += [
            pltpu.VMEM((rows, columns[0]), jnp.float32),
            pltpu.VMEM((4, rows, each), jnp.float32),
            pltpu.VMEM((3, rows, each), jnp.float32),
            pltpu.VMEM(gain_rows.shape, jnp.float32),
            pltpu.VMEM((3,) + gain_rows.shape, jnp.float32),
            pltpu.VMEM(gain_rows.shape, jnp.float32),
            pltpu.VMEM((count - 1,) + gain_rows.shape, jnp.float32),
        ]
        for shape in ((2, half), (2, half - 1), (3,), (3,), (count - 1,)):
            self.scratch += [pltpu.SemaphoreType.DMA(shape)] * 2

    def build(self, inputs, outputs, scratch, count):
        return FinalExchange(inputs, outputs, scratch, count)

    def prepare(self, inputs, outputs):
        pass


def joint_kernel(row_map, extra_count, row_count, sum_count, spreads, rider, count, *refs):
    refs = list(refs)

    def take(number):
        taken = refs[:number]
        del refs[:number]
        return taken

    (partial,) = take(1)
    extras = take(extra_count)
    (gains,) = take(1)
    rider_in = take(rider.inputs)
    gathered = take(1)[0] if spreads else None
    row_outs = take(row_count)
    sum_outs = take(sum_count)
    rider_out = take(rider.outputs)
    near, outgoing, far, send_sems, recv_sems = take(5)
    if spreads:
        spread_send, spread_recv = take(2)
    ring = rider.build(rider_in, rider_out, refs, count)
    ring.sums = sum_outs
    me, mate, across, diagonal = tensor_peers()
    rows_each = partial.shape[1] // chunk_count
    greet([{"tensor": mate}, {"tensor": across}] + ring.targets())
    ring_steps = list(ring.steps())

    def ride():
        if ring_steps:
            ring.advance(ring_steps.pop(0))


    def near_copy(flow, chunk):
        owner = mate if flow else diagonal
        part = pl.ds(chunk * rows_each, rows_each)
        return send(
            partial.at[owner, part], near.at[flow, part], send_sems.at[flow, chunk], recv_sems.at[flow, chunk], {"tensor": mate}
        )

    def far_copy(chunk):
        part = pl.ds(chunk * rows_each, rows_each)
        return send(outgoing.at[part], far.at[part], send_sems.at[2, chunk], recv_sems.at[2, chunk], {"tensor": across})

    for flow in (0, 1):
        for chunk in range(chunk_count):
            near_copy(flow, chunk).start()
    rider.prepare(rider_in, rider_out)
    ride()
    for chunk in range(chunk_count):
        part = pl.ds(chunk * rows_each, rows_each)
        near_copy(0, chunk).wait_recv()
        total = partial[across, part, :].astype(jnp.float32) + near[0, part, :].astype(jnp.float32)
        outgoing[part, :] = total.astype(jnp.bfloat16)
        far_copy(chunk).start()
    ride()
    if spreads:
        spread = Spread(gathered, spread_send, spread_recv, rows_each)
    sums = None
    for chunk in range(chunk_count):
        part = pl.ds(chunk * rows_each, rows_each)
        near_copy(1, chunk).wait_recv()
        total = partial[me, part, :].astype(jnp.float32) + near[1, part, :].astype(jnp.float32)
        far_copy(chunk).wait_recv()
        total = total + far[part, :].astype(jnp.float32)
        given, rows_out, sums_out = row_map(total, [extra[part, :] for extra in extras], gains)
        if spreads:
            gathered[me, part, :] = given.astype(jnp.bfloat16)
            spread.give(chunk)
        for ref, value in zip(row_outs, rows_out):
            ref[part, :] = value.astype(ref.dtype)
        sums = sums_out if sums is None else [held + new for held, new in zip(sums, sums_out)]
        if spreads and chunk > 0:
            spread.forward(chunk - 1)
        if chunk % rider.pace == rider.pace - 1:
            ride()
    for ref, value in zip(sum_outs, sums):
        ref[...] = value
    if spreads:
        spread.forward(chunk_count - 1)
    while ring_steps:
        ride()
    if spreads:
        spread.finish(chunk_count)
    for chunk in range(chunk_count):
        near_copy(0, chunk).wait_send()
        near_copy(1, chunk).wait_send()
        far_copy(chunk).wait_send()
    ring.finish()


def joint(row_map, partial, extras, gains, row_types, sum_count, spreads, rider, count, collective_id):
    rows, width = partial.shape[0] // 4, partial.shape[1]
    outputs = []
    if spreads:
        outputs.append(jax.ShapeDtypeStruct((4, rows, width), jnp.bfloat16))
    outputs += [jax.ShapeDtypeStruct((rows, width), kind) for kind in row_types]
    outputs += [jax.ShapeDtypeStruct((1, width), jnp.float32)] * sum_count
    outputs += rider.shapes
    scratch = [
        pltpu.VMEM((2, rows, width), jnp.bfloat16),
        pltpu.VMEM((rows, width), jnp.bfloat16),
        pltpu.VMEM((rows, width), jnp.bfloat16),
        pltpu.SemaphoreType.DMA((3, chunk_count)),
        pltpu.SemaphoreType.DMA((3, chunk_count)),
    ]
    if spreads:
        scratch += [pltpu.SemaphoreType.DMA((3, chunk_count))] * 2
    scratch += rider.scratch
    found = list(call(
        functools.partial(joint_kernel, row_map, len(extras), len(row_types), sum_count, spreads, rider, count),
        (partial.reshape(4, rows, width),) + tuple(extras) + (gains,) + tuple(rider.arrays),
        outputs,
        scratch,
        collective_id,
    ))
    if spreads:
        found[0] = found[0].reshape(4 * rows, width)
    return found


def branch_map(branch, extras, gains):
    middle = extras[0].astype(jnp.float32) + norm_rows(branch, gains[1:2, :])
    return norm_rows(middle, gains[2:3, :]), [branch, middle], []


def ffn_map(ffn_out, extras, gains):
    middle, cotangent = extras
    outcome = middle + norm_rows(ffn_out, gains[3:4, :])
    grad_ffn, gain_last = norm_pull(ffn_out, gains[3:4, :], cotangent.astype(jnp.float32))
    return grad_ffn, [outcome], [gain_last]


def middle_map(grad_mid_normed, extras, gains):
    middle, branch, cotangent = extras
    pulled, gain_mid = norm_pull(middle, gains[2:3, :], grad_mid_normed)
    grad_middle = cotangent.astype(jnp.float32) + pulled
    grad_branch, gain_branch = norm_pull(branch, gains[1:2, :], grad_middle)
    return grad_branch, [grad_middle], [gain_branch, gain_mid]


def first_map(grad_first_normed, extras, gains):
    tokens, grad_middle = extras
    pulled, gain_first = norm_pull(tokens.astype(jnp.float32), gains[0:1, :], grad_first_normed)
    return None, [grad_middle + pulled], [gain_first]


def hand_over_kernel(count, number, *refs):
    mine = lax.axis_index("dp")
    me = lax.axis_index("tensor")
    sources, targets = refs[: number + 3], refs[number + 3 :]
    for source, target in zip(sources[:number], targets[:number]):
        target[...] = source[...]
    for source, target in zip(sources[number : number + 2], targets[number : number + 2]):
        rows, columns = source.shape
        wide = jnp.concatenate([source[...], jnp.zeros((-rows % 128, columns), source.dtype)], axis=0)
        target[...] = wide.T[:, :rows]
    gain_sum, gains_part, heads_part = sources[number + 2], targets[number + 2], targets[number + 3]
    width = gain_sum.shape[1]
    own = gains_part.shape[1]
    own_head = heads_part.shape[1]
    turned = pltpu.roll(gain_sum[...], (width - mine * own) % width, 1)
    rows_at = lax.broadcasted_iota(jnp.int32, (8, own), 0)
    gains_part[...] = jnp.sum(jnp.where(rows_at == me, turned[:, :own], 0.0), axis=0, keepdims=True)
    turned = pltpu.roll(gain_sum[...], (width - (mine * 4 + me) * own_head) % width, 1)
    heads_part[...] = turned[4:6, :own_head]


def hand_over(straight, turned, gain_sum, count):
    outputs = [jax.ShapeDtypeStruct(array.shape, array.dtype) for array in straight]
    outputs += [jax.ShapeDtypeStruct(array.shape[::-1], array.dtype) for array in turned]
    outputs += [
        jax.ShapeDtypeStruct((1, gain_sum.shape[1] // count), jnp.float32),
        jax.ShapeDtypeStruct((2, turned[0].shape[1] // (4 * count)), jnp.float32),
    ]
    return pl.pallas_call(functools.partial(hand_over_kernel, count, len(straight)), out_shape=outputs)(
        *straight, *turned, gain_sum
    )


def body(
    tokens,
    segments,
    query_weight,
    keyvalue_weight,
    output_weight,
    gate_weight,
    up_weight,
    down_weight,
    norm_gains,
    headnorm_gains,
    cotangent,
):
    head_width = headnorm_gains.shape[1]
    width = tokens.shape[1]
    hidden_width = gate_weight.shape[1]
    count = lax.axis_size("dp")
    own_rows = query_weight.shape[0]
    padded_rows = -(-own_rows // 16) * 16
    seg_tile = segments.reshape(-1, 128)
    rows_all, segment_all, full = opening(
        tokens, seg_tile, norm_gains, (query_weight, keyvalue_weight, output_weight.T), padded_rows, count
    )
    rows_all = rows_all.reshape(-1, width)
    segment_all = segment_all.reshape(-1)

    def join_blocks(blocks):
        return blocks[:, :own_rows].reshape(width, -1)

    def cut_blocks(whole):
        blocks = whole.astype(jnp.bfloat16).reshape(count, own_rows, -1)
        return jnp.pad(blocks, ((0, 0), (0, padded_rows - own_rows), (0, 0)))

    full = join_blocks(full)
    mixed_full = full[:, : 3 * head_width]
    output_full = full[:, 3 * head_width :]
    length = rows_all.shape[0]
    block_rows = min(512, length)
    cosine_table, sine_table = angles(length, head_width)

    def query_map(raw_values, scaling):
        return rotate(norm_rows(raw_values, scaling), cosine_table, sine_table) * score_scale

    def key_map(raw_values, scaling):
        return rotate(norm_rows(raw_values, scaling), cosine_table, sine_table)

    mixed_raw = dot_rows(rows_all, mixed_full)
    query_raw = mixed_raw[:, :head_width]
    keyvalue_raw = mixed_raw[:, head_width:]
    query_rows = query_map(query_raw, headnorm_gains[0]).astype(jnp.bfloat16)
    key_rows = key_map(keyvalue_raw[:, :head_width], headnorm_gains[1]).astype(jnp.bfloat16)
    value_rows = keyvalue_raw[:, head_width:].astype(jnp.bfloat16)

    def masked_scores(row_from, row_to):
        scores = dot_inner(query_rows[row_from:row_to], key_rows[:row_to])
        row_places = row_from + jnp.arange(row_to - row_from)
        key_places = jnp.arange(row_to)
        allowed = (key_places[None, :] <= row_places[:, None]) & (
            segment_all[row_from:row_to][:, None] == segment_all[:row_to][None, :]
        )
        return jnp.where(allowed, scores, -jnp.inf)

    pieces_out = []
    pieces_total = []
    for block_id in range(length // block_rows):
        row_from = block_id * block_rows
        row_to = row_from + block_rows
        scores = masked_scores(row_from, row_to)
        row_peak = jnp.max(scores, axis=-1, keepdims=True)
        raised = jnp.exp(scores - row_peak)
        row_total = jnp.sum(raised, axis=-1, keepdims=True)
        weights_low = (raised / row_total).astype(jnp.bfloat16)
        pieces_out.append(dot_rows(weights_low, value_rows[:row_to]).astype(jnp.bfloat16))
        pieces_total.append(row_peak + jnp.log(row_total))
    attended = jnp.concatenate(pieces_out, axis=0)
    log_totals = jnp.concatenate(pieces_total, axis=0)
    branch_partial = dot_inner(attended, output_full).astype(jnp.bfloat16)
    carried = GatherRider((gate_weight, up_weight, down_weight.T), padded_rows, count)
    mid_all, branch, middle, full = joint(
        branch_map, branch_partial, (tokens,), norm_gains, (jnp.float32, jnp.float32), 0, True, carried, count, 1
    )
    full = join_blocks(full)
    pair_full = full[:, : 2 * hidden_width]
    down_full = full[:, 2 * hidden_width :]
    paired = dot_rows(mid_all, pair_full)
    gating = paired[:, :hidden_width]
    upward = paired[:, hidden_width:]
    idle = IdleRider(count)
    hidden = activate(gating, upward).astype(jnp.bfloat16)
    ffn_partial = dot_inner(hidden, down_full).astype(jnp.bfloat16)
    grad_ffn_all, outcome, gain_last = joint(
        ffn_map, ffn_partial, (middle, cotangent), norm_gains, (jnp.bfloat16,), 1, True, idle, count, 2
    )
    grad_hidden = dot_rows(grad_ffn_all, down_full)
    down_grad = cut_blocks(dot_outer(grad_ffn_all, hidden))
    ignored, pull_active = jax.vjp(activate, gating, upward)
    grad_gating, grad_upward = pull_active(grad_hidden)
    paired_low = jnp.concatenate(
        [grad_gating.astype(jnp.bfloat16), grad_upward.astype(jnp.bfloat16)], axis=1
    )
    mid_partial = dot_inner(paired_low, pair_full).astype(jnp.bfloat16)
    pair_grad = cut_blocks(dot_outer(mid_all, paired_low))
    down_half = hidden_width // 2
    plan = (
        (0, 0, 0, hidden_width, 0, 0),
        (1, 0, hidden_width, hidden_width, 1, 0),
        (0, 1, 0, down_half, 2, 0),
        (1, 1, down_half, down_half, 2, down_half),
    )
    carried = ReduceRider((pair_grad, down_grad), plan, (hidden_width,) * 3, count)
    branch_all, grad_middle, gain_branch, gain_mid, gate_part, up_part, down_part = joint(
        middle_map, mid_partial, (middle, branch, cotangent), norm_gains, (jnp.float32,), 2, True, carried, count, 3
    )
    output_grad = cut_blocks(dot_outer(branch_all, attended))
    grad_attended = dot_rows(branch_all, output_full).astype(jnp.bfloat16)
    grad_query_parts = []
    grad_keys = jnp.zeros((length, head_width), jnp.float32)
    grad_values = jnp.zeros((length, head_width), jnp.float32)
    for block_id in range(length // block_rows):
        row_from = block_id * block_rows
        row_to = row_from + block_rows
        scores = masked_scores(row_from, row_to)
        weights_full = jnp.exp(scores - log_totals[row_from:row_to])
        weights_low = weights_full.astype(jnp.bfloat16)
        grad_block = grad_attended[row_from:row_to]
        grad_weights = dot_inner(grad_block, value_rows[:row_to])
        row_inner = jnp.sum(weights_full * grad_weights, axis=-1, keepdims=True)
        grad_scores = (weights_full * (grad_weights - row_inner)).astype(jnp.bfloat16)
        grad_query_parts.append(dot_rows(grad_scores, key_rows[:row_to]))
        grad_keys = grad_keys.at[:row_to].add(dot_outer(grad_scores, query_rows[row_from:row_to]))
        grad_values = grad_values.at[:row_to].add(dot_outer(weights_low, grad_block))
    grad_query = jnp.concatenate(grad_query_parts, axis=0)
    ignored, pull_query = jax.vjp(query_map, query_raw, headnorm_gains[0])
    grad_query_raw, gain_query = pull_query(grad_query)
    ignored, pull_key = jax.vjp(key_map, keyvalue_raw[:, :head_width], headnorm_gains[1])
    grad_key_raw, gain_key = pull_key(grad_keys)
    mixed_low = jnp.concatenate([grad_query_raw, grad_key_raw, grad_values], axis=1).astype(jnp.bfloat16)
    first_partial = dot_inner(mixed_low, mixed_full).astype(jnp.bfloat16)
    mixed_grad = cut_blocks(dot_outer(rows_all, mixed_low))
    head_rows = jnp.pad(jnp.stack([gain_query, gain_key]), ((0, 2), (0, width - head_width)))
    gain_rows = jnp.concatenate([jnp.zeros_like(gain_last), gain_branch, gain_mid, gain_last, head_rows], axis=0)
    carried = FinalRider(mixed_grad, output_grad, gain_rows, head_width, count)
    grad_tokens, gain_first, query_part, keyvalue_part, output_part, gain_sum = joint(
        first_map, first_partial, (tokens, grad_middle), norm_gains, (jnp.float32,), 1, False, carried, count, 4
    )
    (
        outcome,
        grad_tokens,
        query_part,
        keyvalue_part,
        gate_part,
        up_part,
        output_part,
        down_part,
        gains_part,
        heads_part,
    ) = hand_over(
        (
            outcome,
            grad_tokens,
            query_part[:own_rows],
            keyvalue_part[:own_rows],
            gate_part[:own_rows],
            up_part[:own_rows],
        ),
        (output_part[:own_rows], down_part[:own_rows]),
        gain_sum,
        count,
    )
    return (
        outcome,
        grad_tokens,
        query_part,
        keyvalue_part,
        output_part,
        gate_part,
        up_part,
        down_part,
        gains_part,
        heads_part,
    )


def solution(mesh):
    placed = (
        P(("dp", "tensor"), None),
        P(("dp", "tensor")),
        P("dp", "tensor"),
        P("dp", None),
        P("tensor", "dp"),
        P("dp", "tensor"),
        P("dp", "tensor"),
        P("tensor", "dp"),
        P(),
        P(),
        P(("dp", "tensor"), None),
    )
    return jax.shard_map(
        body,
        mesh=mesh,
        in_specs=placed,
        out_specs=(
            P(("dp", "tensor"), None),
            P(("dp", "tensor"), None),
            P("dp", "tensor"),
            P("dp", "tensor"),
            P("tensor", "dp"),
            P("dp", "tensor"),
            P("dp", "tensor"),
            P("tensor", "dp"),
            P("tensor", "dp"),
            P(None, ("dp", "tensor")),
        ),
        check_vma=False,
    )
```
